32 devices in a mesh: tiles: 2 (over y), rows: 4 (over z), rep: 2 (over x), sub: 2 (over core).
Axes of the slice: x: 2, y: 2, z: 4, core: 2. Of those that a mesh axis runs over, the one named last changes fastest.
Arguments:
- features: float32 [1024, 256], P(('tiles', 'rows')), parts along dimension 0, may hold values from -6 to 6
- center_weight: bfloat16 [256, 256], replicated, may hold values from -0.375 to 0.375
- neighbor_weight: bfloat16 [256, 256], replicated, may hold values from -0.375 to 0.375
- cotangent: float32 [1024, 256], P(('tiles', 'rows')), parts along dimension 0, may hold values from -6 to 6
- tile_rows: int32 [128], P(('tiles', 'rows', 'rep', 'sub')), parts along dimension 0, may hold values from 0 to 7, as said below
- tile_cols: int32 [128], P(('tiles', 'rows', 'rep', 'sub')), parts along dimension 0, may hold values from 0 to 7, as said below
- tile_links: int32 [128, 64, 64], P(('tiles', 'rows', 'rep', 'sub')), parts along dimension 0, may hold values from 0 to 1, as said below
Outputs:
- edge_out: float32 [1024, 256], P(('tiles', 'rows')), parts along dimension 0
- feature_grad: float32 [1024, 256], P(('tiles', 'rows')), parts along dimension 0
- center_grad: float32 [512, 256], P('tiles'), parts along dimension 0
- neighbor_grad: float32 [512, 256], P('tiles'), parts along dimension 0
The draws below stay inside these ranges and needn't reach their ends.
There are 2 independent parts, one for each index of `tiles`. The reference program is written for one: setup_inputs(seed, part) draws one part's arguments, and reference() takes and returns one part's arrays. A program takes and returns all parts, laid end to end along the dimension named above; an argument that names none is the same for every part. Nothing has to cross between parts.
Inputs may be any that keep to these rules, and one draw needn't show every extreme that they name: `tile_rows`: the device at index r of rows, c of rep and s of sub holds 4 tiles; its tile u * 2 + q (u below 2, q below 2) lies in a block row owned by r (blocks r * 2 to r * 2 + 1). `tile_cols`: tile u * 2 + q of the device at index c of rep has its block column owned by the row index u * (size of rep) + c. `tile_links`: 0 or 1. A is symmetric tile by tile: if tile q of section u on the device (r, c, s) joins block a (of owner r) to block b (of owner k), then tile q of section r div (size of rep) on the device (k, r mod (size of rep), s) joins b to a with the transposed links. A tile whose links are all zero is an empty slot.
All inputs are finite; a program needn't handle non-finite values.
Results may differ from the reference program's by a relative error of at most 0.0059.
Values may be sent and summed in bfloat16 or wider, within the bound.
A program may use at most 64 MiB of HBM per device.

```python
import jax
import jax.numpy as jnp
from jax import lax

FEAT = 256
BLOCK = 64
ROW_BLOCKS = 2
TILES_PAIR = 2
NBLK = 8
NPTS = 512
TILE_DEV = 4
N_ROWS = 4
N_REP = 2
N_SUB = 2


def pair_layout(key):
    section_total = N_ROWS // N_REP
    full_shape = (N_ROWS, N_REP, N_SUB, section_total, TILES_PAIR)
    owner_id = jnp.broadcast_to(jnp.arange(N_ROWS, dtype=jnp.int32)[:, None, None, None, None], full_shape)
    rep_id = jnp.broadcast_to(jnp.arange(N_REP, dtype=jnp.int32)[None, :, None, None, None], full_shape)
    sub_id = jnp.broadcast_to(jnp.arange(N_SUB, dtype=jnp.int32)[None, None, :, None, None], full_shape)
    section_id = jnp.broadcast_to(jnp.arange(section_total, dtype=jnp.int32)[None, None, None, :, None], full_shape)
    slot_id = jnp.broadcast_to(jnp.arange(TILES_PAIR, dtype=jnp.int32)[None, None, None, None, :], full_shape)
    other_id = section_id * N_REP + rep_id
    low_id = jnp.minimum(owner_id, other_id)
    high_id = jnp.maximum(owner_id, other_id)
    grid_shape = (N_ROWS, N_ROWS, N_SUB, TILES_PAIR)
    first_block = jax.random.randint(jax.random.fold_in(key, 11), grid_shape, 0, ROW_BLOCKS)
    second_block = jax.random.randint(jax.random.fold_in(key, 12), grid_shape, 0, ROW_BLOCKS)
    low_block = first_block[low_id, high_id, sub_id, slot_id]
    high_block = jnp.where(low_id == high_id, low_block, second_block[low_id, high_id, sub_id, slot_id])
    own_block = jnp.where(owner_id <= other_id, low_block, high_block)
    far_block = jnp.where(owner_id <= other_id, high_block, low_block)
    return (owner_id, other_id, sub_id, slot_id, low_id, high_id, own_block, far_block)


def draw_tile_rows(key, part):
    layout = pair_layout(key)
    return (layout[0] * ROW_BLOCKS + layout[6]).reshape(-1).astype(jnp.int32)


def draw_tile_cols(key, part):
    layout = pair_layout(key)
    return (layout[1] * ROW_BLOCKS + layout[7]).reshape(-1).astype(jnp.int32)


def draw_tile_links(key, part):
    owner_id, other_id, sub_id, slot_id, low_id, high_id, own_block, far_block = pair_layout(key)
    key = jax.random.fold_in(key, 5)
    grid_shape = (N_ROWS, N_ROWS, N_SUB, TILES_PAIR)
    dense_rows = jax.random.randint(jax.random.fold_in(key, 1), (N_ROWS,), 0, 3) == 0
    chance = jax.random.randint(jax.random.fold_in(key, 2), grid_shape, 0, 100)
    busy_pair = dense_rows[low_id] | dense_rows[high_id]
    live_tile = (slot_id == 0) | (low_id == high_id) | (chance[low_id, high_id, sub_id, slot_id] < jnp.where(busy_pair, 90, 20))
    raw_bits = jax.random.randint(jax.random.fold_in(key, 3), grid_shape + (BLOCK, BLOCK), 0, 1000)
    picked = raw_bits[low_id, high_id, sub_id, slot_id]
    link_level = 40 + 25 * (low_id % N_REP + high_id % N_REP) + 40 * sub_id
    link_level = jnp.where(low_id == high_id, 300, link_level)
    joined = picked < link_level[..., None, None]
    joined = jnp.where((owner_id > other_id)[..., None, None], jnp.swapaxes(joined, -1, -2), joined)
    mirrored = joined | jnp.swapaxes(joined, -1, -2)
    joined = jnp.where((low_id == high_id)[..., None, None], mirrored, joined)
    joined = joined & live_tile[..., None, None]
    return joined.astype(jnp.int32).reshape(-1, BLOCK, BLOCK)


def shard_levels(key, shape, cuts, smallest, top_value):
    level, own = 1.0, jax.random.fold_in(key, 6)
    for position, blocks in cuts:
        draws = jnp.exp(jax.random.uniform(jax.random.fold_in(own, position), (blocks,), jnp.float32, smallest / len(cuts), top_value / len(cuts)))
        level = level * jnp.repeat(draws, shape[position] // blocks).reshape([-1 if axis == position else 1 for axis in range(len(shape))])
    return level


def scatter_about(key, extent, width, limit, pieces=(), held_as=jnp.bfloat16):
    values = jax.random.normal(key, extent, jnp.float32) * width
    if len(pieces) > 0:
        values = shard_levels(key, extent, pieces, -0.22, 0.18) * values
    return jnp.clip(values, min=-limit, max=limit).astype(held_as)


def setup_inputs(seed: int = 0, part: int = 0) -> dict:
    arg_keys = jax.random.split(jax.random.key(seed), 8)
    part_splits = jax.random.split(jax.random.fold_in(arg_keys[7], part), 8)
    return {
        "features": scatter_about(part_splits[0], (NPTS, FEAT), 1.0, 6.0, ((0, 4),), jnp.float32),
        "center_weight": scatter_about(arg_keys[1], (FEAT, FEAT), FEAT ** -0.5, 0.375),
        "neighbor_weight": scatter_about(arg_keys[2], (FEAT, FEAT), FEAT ** -0.5, 0.375),
        "cotangent": scatter_about(part_splits[3], (NPTS, FEAT), 1.0, 6.0, ((0, 4),), jnp.float32),
        "tile_rows": draw_tile_rows(jax.random.fold_in(jax.random.fold_in(arg_keys[7], part), 71), part),
        "tile_cols": draw_tile_cols(jax.random.fold_in(jax.random.fold_in(arg_keys[7], part), 71), part),
        "tile_links": draw_tile_links(jax.random.fold_in(jax.random.fold_in(arg_keys[7], part), 71), part),
    }


def silu_slope(argument):
    sigmoid_value = jax.nn.sigmoid(argument)
    return sigmoid_value * (1.0 + argument * (1.0 - sigmoid_value))


def reference(features, center_weight, neighbor_weight, cotangent, tile_rows, tile_cols, tile_links):
    feature_half = features.astype(jnp.bfloat16)
    center = jnp.dot(feature_half, center_weight, preferred_element_type=jnp.float32).astype(jnp.bfloat16)
    neighbor = jnp.dot(feature_half, neighbor_weight, preferred_element_type=jnp.float32).astype(jnp.bfloat16)
    center_full = center.astype(jnp.float32)
    neighbor_full = neighbor.astype(jnp.float32)
    center_blocks = center_full.reshape(NBLK, BLOCK, FEAT)
    neighbor_blocks = neighbor_full.reshape(NBLK, BLOCK, FEAT)
    row_groups = tile_rows.reshape(-1, TILE_DEV)
    col_groups = tile_cols.reshape(-1, TILE_DEV)
    link_groups = tile_links.reshape(-1, TILE_DEV, BLOCK, BLOCK)

    def forward_group(carried, element):
        running, counts = carried
        row_ids, col_ids, link_ints = element
        link_tile = link_ints.astype(jnp.float32)
        pre_act = center_blocks[row_ids][:, :, None, :] + neighbor_blocks[col_ids][:, None, :, :]
        tile_sums = jnp.sum(link_tile[..., None] * jax.nn.silu(pre_act), axis=2)
        running = running.at[row_ids].add(tile_sums)
        counts = counts.at[row_ids].add(jnp.sum(link_tile, axis=2))
        return (running, counts), None

    start = (jnp.zeros((NBLK, BLOCK, FEAT), jnp.float32), jnp.zeros((NBLK, BLOCK), jnp.float32))
    (running, counts), ignored = lax.scan(forward_group, start, (row_groups, col_groups, link_groups))
    degree = counts.reshape(NPTS) + 1.0
    self_pre = center_full + neighbor_full
    edge_out = (running.reshape(NPTS, FEAT) + jax.nn.silu(self_pre)) / degree[:, None]
    scaled = (cotangent / degree[:, None]).astype(jnp.bfloat16)
    scaled_full = scaled.astype(jnp.float32)
    scaled_blocks = scaled_full.reshape(NBLK, BLOCK, FEAT)

    def backward_group(carried, element):
        center_back, neighbor_back = carried
        row_ids, col_ids, link_ints = element
        link_tile = link_ints.astype(jnp.float32)
        pre_act = center_blocks[row_ids][:, :, None, :] + neighbor_blocks[col_ids][:, None, :, :]
        slopes = link_tile[..., None] * scaled_blocks[row_ids][:, :, None, :] * silu_slope(pre_act)
        center_back = center_back.at[row_ids].add(jnp.sum(slopes, axis=2))
        neighbor_back = neighbor_back.at[col_ids].add(jnp.sum(slopes, axis=1))
        return (center_back, neighbor_back), None

    zero_blocks = jnp.zeros((NBLK, BLOCK, FEAT), jnp.float32)
    (center_back, neighbor_back), ignored = lax.scan(backward_group, (zero_blocks, zero_blocks), (row_groups, col_groups, link_groups))
    self_slope = scaled_full * silu_slope(self_pre)
    center_half = (center_back.reshape(NPTS, FEAT) + self_slope).astype(jnp.bfloat16)
    neighbor_half = (neighbor_back.reshape(NPTS, FEAT) + self_slope).astype(jnp.bfloat16)
    feature_grad = jnp.dot(center_half, center_weight.T, preferred_element_type=jnp.float32) + jnp.dot(neighbor_half, neighbor_weight.T, preferred_element_type=jnp.float32)
    center_grad = jnp.dot(feature_half.T, center_half, preferred_element_type=jnp.float32)
    neighbor_grad = jnp.dot(feature_half.T, neighbor_half, preferred_element_type=jnp.float32)
    return (edge_out, feature_grad, center_grad, neighbor_grad)
```

```python
import functools

import jax
import jax.numpy as jnp
from jax import lax
from jax.experimental import pallas as pl
from jax.experimental.pallas import tpu as pltpu
from jax.sharding import PartitionSpec as P

F32 = jnp.float32
BF16 = jnp.bfloat16
MESH = pl.DeviceIdType.MESH
LANES = 4


def dot(a, b, dims=((1,), (0,))):
    return lax.dot_general(a, b, (dims, ((), ())), preferred_element_type=F32)


def kernel(
    sizes,
    rows_s,
    cols_s,
    feat_ref,
    wc_ref,
    wn_ref,
    cot_ref,
    links_ref,
    eo_ref,
    fg_ref,
    cg_ref,
    ng_ref,
    fh_all,
    halves,
    center,
    nown,
    scale,
    degree,
    npanel,
    a4_ref,
    near_s,
    near_d,
    far_acc,
    c_tile,
    s_tile,
    e_acc,
    f_acc,
    near_out,
    far_out,
    near_in,
    far_in,
    cnt,
    eo_all,
    fh_send,
    fh_recv,
    cnt_send,
    cnt_recv,
    near_send,
    near_recv,
    far_send,
    far_recv,
    row_send,
    row_recv,
    grp_send,
    grp_recv,
    eo_send,
    eo_recv,
):
    R, C, S, U, Q, B = sizes
    G = C * S
    points, feat = feat_ref.shape
    nblk = points // B
    sl = points // G
    step = B // LANES
    t_id = lax.axis_index("tiles")
    r = lax.axis_index("rows")
    c = lax.axis_index("rep")
    s = lax.axis_index("sub")
    p = c * S + s

    def dev(row, member):
        return (t_id, row, member // S, member % S)

    barrier = pltpu.get_barrier_semaphore()

    def greet(n, carry):
        other = (r * G + p + n) % (R * G)
        pl.semaphore_signal(
            barrier, inc=1, device_id=dev(other // G, other % G), device_id_type=MESH
        )
        return carry

    lax.fori_loop(1, R * G, greet, 0)

    def own_rows(owner):
        return pl.ds(pl.multiple_of(owner * points, points), points)

    def slice_rows(member):
        return pl.ds(pl.multiple_of(member * sl, sl), sl)

    def hall_rows(owner, member):
        return pl.ds(pl.multiple_of(owner * points + member * sl, sl), sl)

    fh = feat_ref[...].astype(BF16)
    fh_all[own_rows(r), :] = fh

    count = [jnp.zeros((8, B), F32) for _ in range(nblk)]
    for t in range(U * Q):
        tile = links_ref[t].astype(F32)
        a4_ref[t] = jnp.concatenate([tile[m * step : (m + 1) * step] for m in range(LANES)], axis=1)
        row_sum = dot(jnp.ones((8, B), BF16), tile.astype(BF16), ((1,), (1,)))
        block = rows_s[t] - r * nblk
        count = [count[n] + jnp.where(jnp.full(row_sum.shape, block, jnp.int32) == n, row_sum, 0.0) for n in range(nblk)]
    cnt[pl.ds(p, 1)] = jnp.concatenate(count, axis=1)[None]

    pl.semaphore_wait(barrier, R * G - 1)

    def fh_copy(n):
        to = (r + n) % R
        return pltpu.make_async_remote_copy(
            src_ref=fh_all.at[own_rows(r)],
            dst_ref=fh_all.at[own_rows(r)],
            send_sem=fh_send.at[n],
            recv_sem=fh_recv.at[r],
            device_id=dev(to, p),
            device_id_type=MESH,
        )

    def fh_wait(owner):
        pltpu.make_async_remote_copy(
            src_ref=fh_all.at[own_rows(owner)],
            dst_ref=fh_all.at[own_rows(owner)],
            send_sem=fh_send.at[0],
            recv_sem=fh_recv.at[owner],
            device_id=dev(r, p),
            device_id_type=MESH,
        ).wait_recv()

    def member_copy(src, dst, send_sem, recv_sem, n, owner=None):
        return pltpu.make_async_remote_copy(
            src_ref=src,
            dst_ref=dst,
            send_sem=send_sem,
            recv_sem=recv_sem,
            device_id=dev(r if owner is None else owner, (p + n) % G),
            device_id_type=MESH,
        )

    cnt_copies = [
        member_copy(cnt.at[p], cnt.at[p], cnt_send.at[n], cnt_recv.at[p], n) for n in range(1, G)
    ]
    for copy in cnt_copies:
        copy.start()

    @pl.when(r % C == c)
    def _():
        for n in range(1, R):
            fh_copy(n).start()

    cc = dot(fh, wc_ref[...]).astype(BF16).astype(F32) * 0.5
    center[...] = cc
    nn = dot(fh, wn_ref[...]).astype(BF16).astype(F32) * 0.5
    nown[...] = nn

    for n in range(1, G):
        member = (p + n) % G
        member_copy(cnt.at[member], cnt.at[member], cnt_send.at[0], cnt_recv.at[member], 1).wait_recv()
    total = cnt[0]
    for m in range(1, G):
        total = total + cnt[m]
    wide = jnp.concatenate(
        [jnp.transpose(jnp.broadcast_to(total[0:1, h : h + 128], (128, 128))) for h in range(0, points, 128)],
        axis=0,
    )
    deg = jnp.concatenate([wide] * (feat // 128), axis=1) + 1.0
    degree[...] = deg
    scale[...] = (cot_ref[...] / deg).astype(BF16).astype(F32)

    @pl.when(r % C != c)
    def _():
        for n in range(1, R):
            fh_copy(n).start()

    e_acc[...] = jnp.zeros_like(e_acc)
    f_acc[...] = jnp.zeros_like(f_acc)

    lane_m = lax.broadcasted_iota(jnp.int32, (16, LANES * B), 1) // B
    near_mask = jnp.where(
        lax.broadcasted_iota(jnp.int32, (16, LANES * B), 0) == lane_m, 1.0, 0.0
    ).astype(BF16)
    eye_mask = jnp.where(
        lax.broadcasted_iota(jnp.int32, (B, LANES * B), 1) % B
        == lax.broadcasted_iota(jnp.int32, (B, LANES * B), 0),
        1.0,
        0.0,
    ).astype(BF16)

    def in_order(ref):
        return jnp.concatenate(
            [
                jnp.concatenate([ref[k, pl.ds(m, step, stride=8), :] for m in range(LANES)], axis=0)
                for k in range(feat // 128)
            ],
            axis=1,
        )

    def chosen(block, n, value):
        return jnp.where(jnp.full(value.shape, block, jnp.int32) == n, value, 0.0)

    def picked(ref, block):
        value = chosen(block, 0, ref[0:B, :])
        for n in range(1, nblk):
            value = value + chosen(block, n, ref[n * B : (n + 1) * B, :])
        return value

    def section(u):
        owner = u * C + c

        @pl.when(owner != r)
        def _():
            fh_wait(owner)

        npanel[...] = dot(fh_all[own_rows(owner), :], wn_ref[...]).astype(BF16).astype(F32) * 0.5

        for q in range(Q):
            t = u * Q + q
            row_block = rows_s[t] - r * nblk
            col_block = cols_s[t] % nblk
            nval = picked(npanel, col_block).astype(BF16).reshape(B // 16, 16, feat)
            far_acc[...] = jnp.zeros_like(far_acc)
            c_tile[...] = picked(center, row_block)
            s_tile[...] = picked(scale, row_block) * 0.5

            def group(g, carry):
                sil, slo = [], []
                for m in range(LANES):
                    at = pl.ds(g + m * step, 1)
                    crow = jnp.broadcast_to(c_tile[at, :], (16, feat)).astype(BF16)
                    srow = jnp.broadcast_to(s_tile[at, :], (16, feat)).astype(BF16)
                    h = nval + crow[None]
                    th = jnp.tanh(h)
                    one = 1.0 + th
                    sil.append((h * one).reshape(B, feat))
                    slo.append((one * (1.0 + (h - h * th)) * srow[None]).reshape(B, feat))
                sil = jnp.concatenate(sil, axis=0)
                slo = jnp.concatenate(slo, axis=0)
                arow = jnp.broadcast_to(a4_ref[t, pl.ds(g, 1), :], (16, LANES * B)).astype(BF16)
                near_l = near_mask * arow
                far_l = (eye_mask.reshape(B // 16, 16, LANES * B) * arow[None]).reshape(B, LANES * B)
                out_s = dot(near_l, sil)
                out_d = dot(jnp.concatenate([near_l, far_l], axis=0), slo)
                at8 = pl.ds(pl.multiple_of(g * 8, 8), 8)
                for k in range(feat // 128):
                    near_s[k, at8, :] = out_s[0:8, k * 128 : (k + 1) * 128]
                    near_d[k, at8, :] = out_d[0:8, k * 128 : (k + 1) * 128]
                far_acc[...] += out_d[16:]
                return carry

            lax.fori_loop(0, step, group, 0)
            tile_e, tile_c = in_order(near_s), in_order(near_d)
            far = far_acc[...]
            for n in range(nblk):
                block = slice(n * B, (n + 1) * B)
                e_acc[0, block, :] += chosen(row_block, n, tile_e)
                e_acc[1, block, :] += chosen(row_block, n, tile_c)
                if q == 0:
                    f_acc[block, :] = chosen(col_block, n, far)
                else:
                    f_acc[block, :] += chosen(col_block, n, far)

        far_out[u] = f_acc[...].astype(BF16)

        def far_copy(n):
            member = (p + n) % G
            return member_copy(
                far_out.at[u, slice_rows(member)],
                far_in.at[r * S + s],
                far_send.at[u * G + n],
                far_recv.at[r * S + s],
                n,
                owner,
            )

        for n in range(1, G):
            far_copy(n).start()

        @pl.when(owner != r)
        def _():
            far_copy(0).start()

        @pl.when(owner == r)
        def _():
            far_in[pl.ds(r * S + s, 1)] = far_out[u, slice_rows(p), :][None]

        return far_copy

    far_copies = [section(u) for u in range(U)]

    near_out[...] = e_acc[...].astype(BF16)
    near_copies = [
        member_copy(
            near_out.at[:, slice_rows((p + n) % G)],
            near_in.at[p],
            near_send.at[n],
            near_recv.at[p],
            n,
        )
        for n in range(1, G)
    ]
    for copy in near_copies:
        copy.start()

    mine = slice_rows(p)
    cs, ns = center[mine, :], nown[mine, :]
    sc, dg = scale[mine, :], degree[mine, :]
    self_h = cs + ns
    self_t = jnp.tanh(self_h)
    self_silu = self_h * (1.0 + self_t)
    self_slope = sc * 0.5 * (1.0 + self_t) * (1.0 + self_h * (1.0 - self_t))
    e_sum = e_acc[0, mine, :] + self_silu
    c_sum = e_acc[1, mine, :] + self_slope
    for n in range(1, G):
        member = (p + n) % G
        member_copy(
            near_out.at[:, mine], near_in.at[member], near_send.at[0], near_recv.at[member], 1
        ).wait_recv()
        arrived = near_in[pl.ds(member, 1)][0]
        e_sum = e_sum + arrived[0].astype(F32)
        c_sum = c_sum + arrived[1].astype(F32)
    eo_all[mine, :] = (e_sum / dg).astype(BF16)
    eo_copies = [
        member_copy(eo_all.at[mine], eo_all.at[mine], eo_send.at[n], eo_recv.at[p], n)
        for n in range(1, G)
    ]
    for copy in eo_copies:
        copy.start()

    n_sum = self_slope
    for row in range(R):
        for sub in range(S):
            slot = row * S + sub
            here = (row == r) & (sub == s) & (r % C == c)

            @pl.when(jnp.logical_not(here))
            def _():
                member_copy(
                    far_out.at[0, mine], far_in.at[slot], far_send.at[0], far_recv.at[slot], 1
                ).wait_recv()

            n_sum = n_sum + far_in[slot].astype(F32)

    def own_part(owner, member):
        return halves.at[:, hall_rows(owner, member)]

    halves[0, hall_rows(r, p), :] = c_sum.astype(BF16)
    halves[1, hall_rows(r, p), :] = n_sum.astype(BF16)

    def row_copy(n):
        return pltpu.make_async_remote_copy(
            src_ref=own_part(r, p),
            dst_ref=own_part(r, p),
            send_sem=row_send.at[n],
            recv_sem=row_recv.at[r],
            device_id=dev((r + n) % R, p),
            device_id_type=MESH,
        )

    def relay_copy(n_row, n):
        owner = (r + n_row) % R
        return member_copy(
            own_part(owner, p),
            own_part(owner, p),
            grp_send.at[n_row * G + n],
            grp_recv.at[owner * G + p],
            n,
        )

    for n in range(1, R):
        row_copy(n).start()
    for n in range(1, G):
        relay_copy(0, n).start()
    for n_row in range(1, R):
        owner = (r + n_row) % R
        pltpu.make_async_remote_copy(
            src_ref=own_part(owner, p),
            dst_ref=own_part(owner, p),
            send_sem=row_send.at[0],
            recv_sem=row_recv.at[owner],
            device_id=dev(r, p),
            device_id_type=MESH,
        ).wait_recv()
        for n in range(1, G):
            relay_copy(n_row, n).start()

    for n in range(1, G):
        member = (p + n) % G
        rows = slice_rows(member)
        member_copy(eo_all.at[rows], eo_all.at[rows], eo_send.at[0], eo_recv.at[member], 1).wait_recv()
    eo_ref[...] = eo_all[...].astype(F32)

    def grp_wait(owner):
        for n in range(1, G):
            member = (p + n) % G
            member_copy(
                own_part(owner, member),
                own_part(owner, member),
                grp_send.at[0],
                grp_recv.at[owner * G + member],
                1,
            ).wait_recv()

    grp_wait(r)
    fg_ref[...] = dot(halves[0, own_rows(r), :], wc_ref[...], ((1,), (1,))) + dot(
        halves[1, own_rows(r), :], wn_ref[...], ((1,), (1,))
    )
    for n in range(1, R):
        owner = (r + n) % R

        @pl.when(owner % C != c)
        def _():
            fh_wait(owner)

    for n in range(1, R):
        grp_wait((r + n) % R)
    cg_ref[...] = dot(fh_all[...], halves[0], ((0,), (0,)))
    ng_ref[...] = dot(fh_all[...], halves[1], ((0,), (0,)))

    for n in range(1, R):
        fh_copy(n).wait_send()
        row_copy(n).wait_send()
    for copy in cnt_copies + near_copies + eo_copies:
        copy.wait_send()
    for n_row in range(R):
        for n in range(1, G):
            relay_copy(n_row, n).wait_send()
    for u in range(U):
        for n in range(1, G):
            far_copies[u](n).wait_send()

        @pl.when(u * C + c != r)
        def _():
            far_copies[u](0).wait_send()


def body(features, center_weight, neighbor_weight, cotangent, tile_rows, tile_cols, tile_links):
    R, C, S = lax.axis_size("rows"), lax.axis_size("rep"), lax.axis_size("sub")
    U = R // C
    T, B = tile_rows.shape[0], tile_links.shape[1]
    points, feat = features.shape
    G = C * S
    sl = points // G
    sizes = (R, C, S, U, T // U, B)
    step = B // LANES
    dma = pltpu.SemaphoreType.DMA
    vm = pltpu.VMEM
    out = jax.ShapeDtypeStruct
    return pl.pallas_call(
        functools.partial(kernel, sizes),
        out_shape=(
            out((points, feat), F32),
            out((points, feat), F32),
            out((feat, feat), F32),
            out((feat, feat), F32),
        ),
        in_specs=[pl.BlockSpec(memory_space=pltpu.SMEM)] * 2
        + [pl.BlockSpec(memory_space=pltpu.VMEM)] * 5,
        out_specs=[pl.BlockSpec(memory_space=pltpu.VMEM)] * 4,
        scratch_shapes=[
            vm((R * points, feat), BF16),
            vm((2, R * points, feat), BF16),
            vm((points, feat), F32),
            vm((points, feat), F32),
            vm((points, feat), F32),
            vm((points, feat), F32),
            vm((points, feat), F32),
            vm((T, step, LANES * B), F32),
            vm((feat // 128, step * 8, 128), F32),
            vm((feat // 128, step * 8, 128), F32),
            vm((B, feat), F32),
            vm((B, feat), F32),
            vm((B, feat), F32),
            vm((2, points, feat), F32),
            vm((points, feat), F32),
            vm((2, points, feat), BF16),
            vm((U, points, feat), BF16),
            vm((G, 2, sl, feat), BF16),
            vm((R * S, sl, feat), BF16),
            vm((G, 8, points), F32),
            vm((points, feat), BF16),
            dma((R,)),
            dma((R,)),
            dma((G,)),
            dma((G,)),
            dma((G,)),
            dma((G,)),
            dma((U * G,)),
            dma((R * S,)),
            dma((R,)),
            dma((R,)),
            dma((R * G,)),
            dma((R * G,)),
            dma((G,)),
            dma((G,)),
        ],
        compiler_params=pltpu.CompilerParams(
            collective_id=0, has_side_effects=True, vmem_limit_bytes=48 * 1024 * 1024
        ),
    )(tile_rows, tile_cols, features, center_weight, neighbor_weight, cotangent, tile_links)


def solution(mesh):
    in_specs = (
        P(("tiles", "rows"), None),
        P(),
        P(),
        P(("tiles", "rows"), None),
        P(("tiles", "rows", "rep", "sub")),
        P(("tiles", "rows", "rep", "sub")),
        P(("tiles", "rows", "rep", "sub"), None, None),
    )
    out_specs = (
        P(("tiles", "rows"), None),
        P(("tiles", "rows"), None),
        P("tiles", None),
        P("tiles", None),
    )
    return jax.shard_map(body, mesh=mesh, in_specs=in_specs, out_specs=out_specs, check_vma=False)
```

```python
import functools

import jax
import jax.numpy as jnp
from jax import lax
from jax.experimental import pallas as pl
from jax.experimental.pallas import tpu as pltpu
from jax.sharding import PartitionSpec as P

F32 = jnp.float32
BF16 = jnp.bfloat16
MESH = pl.DeviceIdType.MESH
LANES = 4


def dot(a, b, dims=((1,), (0,))):
    return lax.dot_general(a, b, (dims, ((), ())), preferred_element_type=F32)


def kernel(
    sizes,
    rows_h,
    cols_h,
    feat_h,
    wc_h,
    wn_h,
    cot_h,
    links_h,
    eo_ref,
    fg_ref,
    cg_ref,
    ng_ref,
    rows_s,
    cols_s,
    feat_ref,
    wc_ref,
    wn_ref,
    cot_ref,
    links_ref,
    in_sem,
    fh_all,
    halves,
    center,
    nown,
    scale,
    degree,
    npanel,
    a4_ref,
    near_s,
    near_d,
    far_acc,
    c_tile,
    s_tile,
    e_acc,
    f_acc,
    near_out,
    far_out,
    near_in,
    far_in,
    cnt,
    eo_all,
    fh_send,
    fh_recv,
    cnt_send,
    cnt_recv,
    near_send,
    near_recv,
    far_send,
    far_recv,
    row_send,
    row_recv,
    grp_send,
    grp_recv,
    eo_send,
    eo_recv,
):
    R, C, S, U, Q, B = sizes
    G = C * S
    points, feat = feat_ref.shape
    nblk = points // B
    sl = points // G
    step = B // LANES
    t_id = lax.axis_index("tiles")
    r = lax.axis_index("rows")
    c = lax.axis_index("rep")
    s = lax.axis_index("sub")
    p = c * S + s

    def dev(row, member):
        return (t_id, row, member // S, member % S)

    loads = [
        pltpu.make_async_copy(src, dst, in_sem.at[k])
        for k, (src, dst) in enumerate(
            (
                (feat_h, feat_ref),
                (links_h, links_ref),
                (rows_h, rows_s),
                (cols_h, cols_s),
                (wc_h, wc_ref),
                (wn_h, wn_ref),
                (cot_h, cot_ref),
            )
        )
    ]
    for load in loads:
        load.start()

    barrier = pltpu.get_barrier_semaphore()

    def greet(n, carry):
        other = (r * G + p + n) % (R * G)
        pl.semaphore_signal(
            barrier, inc=1, device_id=dev(other // G, other % G), device_id_type=MESH
        )
        return carry

    lax.fori_loop(1, R * G, greet, 0)

    def own_rows(owner):
        return pl.ds(pl.multiple_of(owner * points, points), points)

    def slice_rows(member):
        return pl.ds(pl.multiple_of(member * sl, sl), sl)

    def hall_rows(owner, member):
        return pl.ds(pl.multiple_of(owner * points + member * sl, sl), sl)

    loads[0].wait()
    fh = feat_ref[...].astype(BF16)
    fh_all[own_rows(r), :] = fh

    for load in loads[1:4]:
        load.wait()

    count = [jnp.zeros((8, B), F32) for _ in range(nblk)]
    for t in range(U * Q):
        tile = links_ref[t].astype(F32)
        a4_ref[t] = jnp.concatenate([tile[m * step : (m + 1) * step] for m in range(LANES)], axis=1)
        row_sum = dot(jnp.ones((8, B), BF16), tile.astype(BF16), ((1,), (1,)))
        block = rows_s[t] - r * nblk
        count = [count[n] + jnp.where(jnp.full(row_sum.shape, block, jnp.int32) == n, row_sum, 0.0) for n in range(nblk)]
    cnt[pl.ds(p, 1)] = jnp.concatenate(count, axis=1)[None]

    pl.semaphore_wait(barrier, R * G - 1)

    def fh_copy(n):
        to = (r + n) % R
        return pltpu.make_async_remote_copy(
            src_ref=fh_all.at[own_rows(r)],
            dst_ref=fh_all.at[own_rows(r)],
            send_sem=fh_send.at[n],
            recv_sem=fh_recv.at[r],
            device_id=dev(to, p),
            device_id_type=MESH,
        )

    def fh_wait(owner):
        pltpu.make_async_remote_copy(
            src_ref=fh_all.at[own_rows(owner)],
            dst_ref=fh_all.at[own_rows(owner)],
            send_sem=fh_send.at[0],
            recv_sem=fh_recv.at[owner],
            device_id=dev(r, p),
            device_id_type=MESH,
        ).wait_recv()

    def member_copy(src, dst, send_sem, recv_sem, n, owner=None):
        return pltpu.make_async_remote_copy(
            src_ref=src,
            dst_ref=dst,
            send_sem=send_sem,
            recv_sem=recv_sem,
            device_id=dev(r if owner is None else owner, (p + n) % G),
            device_id_type=MESH,
        )

    cnt_copies = [
        member_copy(cnt.at[p], cnt.at[p], cnt_send.at[n], cnt_recv.at[p], n) for n in range(1, G)
    ]
    for copy in cnt_copies:
        copy.start()

    @pl.when(r % C == c)
    def _():
        for n in range(1, R):
            fh_copy(n).start()

    for load in loads[4:]:
        load.wait()
    cc = dot(fh, wc_ref[...]).astype(BF16).astype(F32) * 0.5
    center[...] = cc
    nn = dot(fh, wn_ref[...]).astype(BF16).astype(F32) * 0.5
    nown[...] = nn

    for n in range(1, G):
        member = (p + n) % G
        member_copy(cnt.at[member], cnt.at[member], cnt_send.at[0], cnt_recv.at[member], 1).wait_recv()
    total = cnt[0]
    for m in range(1, G):
        total = total + cnt[m]
    wide = jnp.concatenate(
        [jnp.transpose(jnp.broadcast_to(total[0:1, h : h + 128], (128, 128))) for h in range(0, points, 128)],
        axis=0,
    )
    deg = jnp.concatenate([wide] * (feat // 128), axis=1) + 1.0
    degree[...] = deg
    scale[...] = (cot_ref[...] / deg).astype(BF16).astype(F32)

    @pl.when(r % C != c)
    def _():
        for n in range(1, R):
            fh_copy(n).start()

    e_acc[...] = jnp.zeros_like(e_acc)
    f_acc[...] = jnp.zeros_like(f_acc)

    lane_m = lax.broadcasted_iota(jnp.int32, (16, LANES * B), 1) // B
    near_mask = jnp.where(
        lax.broadcasted_iota(jnp.int32, (16, LANES * B), 0) == lane_m, 1.0, 0.0
    ).astype(BF16)
    eye_mask = jnp.where(
        lax.broadcasted_iota(jnp.int32, (B, LANES * B), 1) % B
        == lax.broadcasted_iota(jnp.int32, (B, LANES * B), 0),
        1.0,
        0.0,
    ).astype(BF16)

    def in_order(ref):
        return jnp.concatenate(
            [
                jnp.concatenate([ref[k, pl.ds(m, step, stride=8), :] for m in range(LANES)], axis=0)
                for k in range(feat // 128)
            ],
            axis=1,
        )

    def chosen(block, n, value):
        return jnp.where(jnp.full(value.shape, block, jnp.int32) == n, value, 0.0)

    def picked(ref, block):
        value = chosen(block, 0, ref[0:B, :])
        for n in range(1, nblk):
            value = value + chosen(block, n, ref[n * B : (n + 1) * B, :])
        return value

    def section(u):
        owner = u * C + c

        @pl.when(owner != r)
        def _():
            fh_wait(owner)

        npanel[...] = dot(fh_all[own_rows(owner), :], wn_ref[...]).astype(BF16).astype(F32) * 0.5

        for q in range(Q):
            t = u * Q + q
            row_block = rows_s[t] - r * nblk
            col_block = cols_s[t] % nblk
            nval = picked(npanel, col_block).astype(BF16).reshape(B // 16, 16, feat)
            far_acc[...] = jnp.zeros_like(far_acc)
            c_tile[...] = picked(center, row_block)
            s_tile[...] = picked(scale, row_block) * 0.5

            def group(g, carry):
                sil, slo = [], []
                for m in range(LANES):
                    at = pl.ds(g + m * step, 1)
                    crow = jnp.broadcast_to(c_tile[at, :], (16, feat)).astype(BF16)
                    srow = jnp.broadcast_to(s_tile[at, :], (16, feat)).astype(BF16)
                    h = nval + crow[None]
                    th = jnp.tanh(h)
                    one = 1.0 + th
                    sil.append((h * one).reshape(B, feat))
                    slo.append((one * (1.0 + h * (1.0 - th)) * srow[None]).reshape(B, feat))
                sil = jnp.concatenate(sil, axis=0)
                slo = jnp.concatenate(slo, axis=0)
                arow = jnp.broadcast_to(a4_ref[t, pl.ds(g, 1), :], (16, LANES * B)).astype(BF16)
                near_l = near_mask * arow
                far_l = (eye_mask.reshape(B // 16, 16, LANES * B) * arow[None]).reshape(B, LANES * B)
                out_s = dot(near_l, sil)
                out_d = dot(jnp.concatenate([near_l, far_l], axis=0), slo)
                at8 = pl.ds(pl.multiple_of(g * 8, 8), 8)
                for k in range(feat // 128):
                    near_s[k, at8, :] = out_s[0:8, k * 128 : (k + 1) * 128]
                    near_d[k, at8, :] = out_d[0:8, k * 128 : (k + 1) * 128]
                far_acc[...] += out_d[16:]
                return carry

            lax.fori_loop(0, step, group, 0, unroll=4)
            tile_e, tile_c = in_order(near_s), in_order(near_d)
            far = far_acc[...]
            for n in range(nblk):
                block = slice(n * B, (n + 1) * B)
                e_acc[0, block, :] += chosen(row_block, n, tile_e)
                e_acc[1, block, :] += chosen(row_block, n, tile_c)
                if q == 0:
                    f_acc[block, :] = chosen(col_block, n, far)
                else:
                    f_acc[block, :] += chosen(col_block, n, far)

        far_out[u] = f_acc[...].astype(BF16)

        def far_copy(n):
            member = (p + n) % G
            return member_copy(
                far_out.at[u, slice_rows(member)],
                far_in.at[r * S + s],
                far_send.at[u * G + n],
                far_recv.at[r * S + s],
                n,
                owner,
            )

        for n in range(1, G):
            far_copy(n).start()

        @pl.when(owner != r)
        def _():
            far_copy(0).start()

        @pl.when(owner == r)
        def _():
            far_in[pl.ds(r * S + s, 1)] = far_out[u, slice_rows(p), :][None]

        return far_copy

    far_copies = [section(u) for u in range(U)]

    near_out[...] = e_acc[...].astype(BF16)
    near_copies = [
        member_copy(
            near_out.at[:, slice_rows((p + n) % G)],
            near_in.at[p],
            near_send.at[n],
            near_recv.at[p],
            n,
        )
        for n in range(1, G)
    ]
    for copy in near_copies:
        copy.start()

    mine = slice_rows(p)
    cs, ns = center[mine, :], nown[mine, :]
    sc, dg = scale[mine, :], degree[mine, :]
    self_h = cs + ns
    self_t = jnp.tanh(self_h)
    self_silu = self_h * (1.0 + self_t)
    self_slope = sc * 0.5 * (1.0 + self_t) * (1.0 + self_h * (1.0 - self_t))
    e_sum = e_acc[0, mine, :] + self_silu
    c_sum = e_acc[1, mine, :] + self_slope
    for n in range(1, G):
        member = (p + n) % G
        member_copy(
            near_out.at[:, mine], near_in.at[member], near_send.at[0], near_recv.at[member], 1
        ).wait_recv()
        arrived = near_in[pl.ds(member, 1)][0]
        e_sum = e_sum + arrived[0].astype(F32)
        c_sum = c_sum + arrived[1].astype(F32)
    eo_all[mine, :] = (e_sum / dg).astype(BF16)
    eo_copies = [
        member_copy(eo_all.at[mine], eo_all.at[mine], eo_send.at[n], eo_recv.at[p], n)
        for n in range(1, G)
    ]
    for copy in eo_copies:
        copy.start()

    n_sum = self_slope
    for row in range(R):
        for sub in range(S):
            slot = row * S + sub
            here = (row == r) & (sub == s) & (r % C == c)

            @pl.when(jnp.logical_not(here))
            def _():
                member_copy(
                    far_out.at[0, mine], far_in.at[slot], far_send.at[0], far_recv.at[slot], 1
                ).wait_recv()

            n_sum = n_sum + far_in[slot].astype(F32)

    def own_part(owner, member):
        return halves.at[:, hall_rows(owner, member)]

    halves[0, hall_rows(r, p), :] = c_sum.astype(BF16)
    halves[1, hall_rows(r, p), :] = n_sum.astype(BF16)

    def row_copy(n):
        return pltpu.make_async_remote_copy(
            src_ref=own_part(r, p),
            dst_ref=own_part(r, p),
            send_sem=row_send.at[n],
            recv_sem=row_recv.at[r],
            device_id=dev((r + n) % R, p),
            device_id_type=MESH,
        )

    def part_wait(owner, member, sems, at):
        pltpu.make_async_remote_copy(
            src_ref=own_part(owner, member),
            dst_ref=own_part(owner, member),
            send_sem=row_send.at[0],
            recv_sem=sems.at[at],
            device_id=dev(r, p),
            device_id_type=MESH,
        ).wait_recv()

    def part_copy(n_row, n, via, chips, cores):
        owner = (r + n_row) % R
        member = ((c + via) % C) * S + s
        return pltpu.make_async_remote_copy(
            src_ref=own_part(owner, member),
            dst_ref=own_part(owner, member),
            send_sem=grp_send.at[n_row * G + n],
            recv_sem=grp_recv.at[owner * G + member],
            device_id=(t_id, r, (c + chips) % C, (s + cores) % S),
            device_id_type=MESH,
        )

    def across(n_row):
        return [part_copy(n_row, k - 1, 0, k, 0) for k in range(1, C)]

    def inside(n_row, via):
        return [part_copy(n_row, C + via * (S - 1) + k - 2, via, 0, k) for k in range(1, S)]

    for n in range(1, R):
        row_copy(n).start()
    for copy in across(0) + inside(0, 0):
        copy.start()
    for n_row in range(R):
        owner = (r + n_row) % R
        if n_row > 0:
            part_wait(owner, p, row_recv, owner)
            for copy in across(n_row) + inside(n_row, 0):
                copy.start()
        before = n_row - 1
        if before >= 0:
            owner = (r + before) % R
            for via in range(1, C):
                member = ((c + via) % C) * S + s
                part_wait(owner, member, grp_recv, owner * G + member)
                for copy in inside(before, via):
                    copy.start()
    last = (r + R - 1) % R
    for via in range(1, C):
        member = ((c + via) % C) * S + s
        part_wait(last, member, grp_recv, last * G + member)
        for copy in inside(R - 1, via):
            copy.start()

    for n in range(1, G):
        member = (p + n) % G
        rows = slice_rows(member)
        member_copy(eo_all.at[rows], eo_all.at[rows], eo_send.at[0], eo_recv.at[member], 1).wait_recv()
    eo_ref[...] = eo_all[...].astype(F32)

    def grp_wait(owner):
        for via in range(C):
            for k in range(1, S):
                member = ((c + via) % C) * S + (s + k) % S
                part_wait(owner, member, grp_recv, owner * G + member)

    grp_wait(r)
    fg_ref[...] = dot(halves[0, own_rows(r), :], wc_ref[...], ((1,), (1,))) + dot(
        halves[1, own_rows(r), :], wn_ref[...], ((1,), (1,))
    )
    for n in range(1, R):
        owner = (r + n) % R

        @pl.when(owner % C != c)
        def _():
            fh_wait(owner)

    for n in range(1, R):
        grp_wait((r + n) % R)
    cg_ref[...] = dot(fh_all[...], halves[0], ((0,), (0,)))
    ng_ref[...] = dot(fh_all[...], halves[1], ((0,), (0,)))

    for n in range(1, R):
        fh_copy(n).wait_send()
        row_copy(n).wait_send()
    for copy in cnt_copies + near_copies + eo_copies:
        copy.wait_send()
    for n_row in range(R):
        for copy in across(n_row) + [one for via in range(C) for one in inside(n_row, via)]:
            copy.wait_send()
    for u in range(U):
        for n in range(1, G):
            far_copies[u](n).wait_send()

        @pl.when(u * C + c != r)
        def _():
            far_copies[u](0).wait_send()


def body(features, center_weight, neighbor_weight, cotangent, tile_rows, tile_cols, tile_links):
    R, C, S = lax.axis_size("rows"), lax.axis_size("rep"), lax.axis_size("sub")
    U = R // C
    T, B = tile_rows.shape[0], tile_links.shape[1]
    points, feat = features.shape
    G = C * S
    sl = points // G
    sizes = (R, C, S, U, T // U, B)
    step = B // LANES
    dma = pltpu.SemaphoreType.DMA
    vm = pltpu.VMEM
    out = jax.ShapeDtypeStruct
    return pl.pallas_call(
        functools.partial(kernel, sizes),
        out_shape=(
            out((points, feat), F32),
            out((points, feat), F32),
            out((feat, feat), F32),
            out((feat, feat), F32),
        ),
        in_specs=[pl.BlockSpec(memory_space=pltpu.HBM)] * 7,
        out_specs=[pl.BlockSpec(memory_space=pltpu.VMEM)] * 4,
        scratch_shapes=[
            pltpu.SMEM((T,), jnp.int32),
            pltpu.SMEM((T,), jnp.int32),
            vm((points, feat), F32),
            vm((feat, feat), BF16),
            vm((feat, feat), BF16),
            vm((points, feat), F32),
            vm((T, B, B), jnp.int32),
            dma((7,)),
            vm((R * points, feat), BF16),
            vm((2, R * points, feat), BF16),
            vm((points, feat), F32),
            vm((points, feat), F32),
            vm((points, feat), F32),
            vm((points, feat), F32),
            vm((points, feat), F32),
            vm((T, step, LANES * B), F32),
            vm((feat // 128, step * 8, 128), F32),
            vm((feat // 128, step * 8, 128), F32),
            vm((B, feat), F32),
            vm((B, feat), F32),
            vm((B, feat), F32),
            vm((2, points, feat), F32),
            vm((points, feat), F32),
            vm((2, points, feat), BF16),
            vm((U, points, feat), BF16),
            vm((G, 2, sl, feat), BF16),
            vm((R * S, sl, feat), BF16),
            vm((G, 8, points), F32),
            vm((points, feat), BF16),
            dma((R,)),
            dma((R,)),
            dma((G,)),
            dma((G,)),
            dma((G,)),
            dma((G,)),
            dma((U * G,)),
            dma((R * S,)),
            dma((R,)),
            dma((R,)),
            dma((R * G,)),
            dma((R * G,)),
            dma((G,)),
            dma((G,)),
        ],
        compiler_params=pltpu.CompilerParams(
            collective_id=0, has_side_effects=True, vmem_limit_bytes=48 * 1024 * 1024
        ),
    )(tile_rows, tile_cols, features, center_weight, neighbor_weight, cotangent, tile_links)


def solution(mesh):
    in_specs = (
        P(("tiles", "rows"), None),
        P(),
        P(),
        P(("tiles", "rows"), None),
        P(("tiles", "rows", "rep", "sub")),
        P(("tiles", "rows", "rep", "sub")),
        P(("tiles", "rows", "rep", "sub"), None, None),
    )
    out_specs = (
        P(("tiles", "rows"), None),
        P(("tiles", "rows"), None),
        P("tiles", None),
        P("tiles", None),
    )
    return jax.shard_map(body, mesh=mesh, in_specs=in_specs, out_specs=out_specs, check_vma=False)
```

```python
import functools

import jax
import jax.numpy as jnp
from jax import lax
from jax.experimental import pallas as pl
from jax.experimental.pallas import tpu as pltpu
from jax.sharding import PartitionSpec as P

F32 = jnp.float32
BF16 = jnp.bfloat16
MESH = pl.DeviceIdType.MESH
LANES = 4


def dot(a, b, dims=((1,), (0,))):
    return lax.dot_general(a, b, (dims, ((), ())), preferred_element_type=F32)


def kernel(
    sizes,
    rows_h,
    cols_h,
    feat_h,
    wc_h,
    wn_h,
    cot_h,
    links_h,
    eo_ref,
    fg_ref,
    cg_ref,
    ng_ref,
    rows_s,
    cols_s,
    feat_ref,
    wc_ref,
    wn_ref,
    cot_ref,
    links_ref,
    in_sem,
    fh_all,
    halves,
    center,
    nown,
    scale,
    degree,
    npanel,
    a4_ref,
    near_s,
    near_d,
    far_acc,
    c_tile,
    s_tile,
    e_acc,
    f_acc,
    near_out,
    far_out,
    near_in,
    far_in,
    cnt,
    eo_all,
    fh_send,
    fh_recv,
    cnt_send,
    cnt_recv,
    near_send,
    near_recv,
    far_send,
    far_recv,
    row_send,
    row_recv,
    grp_send,
    grp_recv,
    eo_send,
    eo_recv,
):
    R, C, S, U, Q, B = sizes
    G = C * S
    points, feat = feat_ref.shape
    nblk = points // B
    sl = points // G
    step = B // LANES
    t_id = lax.axis_index("tiles")
    r = lax.axis_index("rows")
    c = lax.axis_index("rep")
    s = lax.axis_index("sub")
    p = c * S + s

    def dev(row, member):
        return (t_id, row, member // S, member % S)

    loads = [
        pltpu.make_async_copy(src, dst, in_sem.at[k])
        for k, (src, dst) in enumerate(
            (
                (feat_h, feat_ref),
                (links_h, links_ref),
                (rows_h, rows_s),
                (cols_h, cols_s),
                (wc_h, wc_ref),
                (wn_h, wn_ref),
                (cot_h, cot_ref),
            )
        )
    ]
    for load in loads:
        load.start()

    barrier = pltpu.get_barrier_semaphore()

    def greet(n, carry):
        other = (r * G + p + n) % (R * G)
        pl.semaphore_signal(
            barrier, inc=1, device_id=dev(other // G, other % G), device_id_type=MESH
        )
        return carry

    lax.fori_loop(1, R * G, greet, 0)

    def own_rows(owner):
        return pl.ds(pl.multiple_of(owner * points, points), points)

    def slice_rows(member):
        return pl.ds(pl.multiple_of(member * sl, sl), sl)

    def hall_rows(owner, member):
        return pl.ds(pl.multiple_of(owner * points + member * sl, sl), sl)

    loads[0].wait()
    fh = feat_ref[...].astype(BF16)
    fh_all[own_rows(r), :] = fh

    for load in loads[1:4]:
        load.wait()

    count = [jnp.zeros((8, B), F32) for _ in range(nblk)]
    for t in range(U * Q):
        tile = links_ref[t].astype(F32)
        a4_ref[t] = jnp.concatenate([tile[m * step : (m + 1) * step] for m in range(LANES)], axis=1)
        row_sum = dot(jnp.ones((8, B), BF16), tile.astype(BF16), ((1,), (1,)))
        block = rows_s[t] - r * nblk
        count = [count[n] + jnp.where(jnp.full(row_sum.shape, block, jnp.int32) == n, row_sum, 0.0) for n in range(nblk)]
    cnt[pl.ds(p, 1)] = jnp.concatenate(count, axis=1)[None]

    pl.semaphore_wait(barrier, R * G - 1)

    def fh_copy(n):
        to = (r + n) % R
        return pltpu.make_async_remote_copy(
            src_ref=fh_all.at[own_rows(r)],
            dst_ref=fh_all.at[own_rows(r)],
            send_sem=fh_send.at[n],
            recv_sem=fh_recv.at[r],
            device_id=dev(to, p),
            device_id_type=MESH,
        )

    def fh_wait(owner):
        pltpu.make_async_remote_copy(
            src_ref=fh_all.at[own_rows(owner)],
            dst_ref=fh_all.at[own_rows(owner)],
            send_sem=fh_send.at[0],
            recv_sem=fh_recv.at[owner],
            device_id=dev(r, p),
            device_id_type=MESH,
        ).wait_recv()

    def member_copy(src, dst, send_sem, recv_sem, n, owner=None):
        return pltpu.make_async_remote_copy(
            src_ref=src,
            dst_ref=dst,
            send_sem=send_sem,
            recv_sem=recv_sem,
            device_id=dev(r if owner is None else owner, (p + n) % G),
            device_id_type=MESH,
        )

    cnt_copies = [
        member_copy(cnt.at[p], cnt.at[p], cnt_send.at[n], cnt_recv.at[p], n) for n in range(1, G)
    ]
    for copy in cnt_copies:
        copy.start()

    @pl.when(r % C == c)
    def _():
        for n in range(1, R):
            fh_copy(n).start()

    for load in loads[4:]:
        load.wait()
    cc = dot(fh, wc_ref[...]).astype(BF16).astype(F32) * 0.5
    center[...] = cc
    nn = dot(fh, wn_ref[...]).astype(BF16).astype(F32) * 0.5
    nown[...] = nn

    for n in range(1, G):
        member = (p + n) % G
        member_copy(cnt.at[member], cnt.at[member], cnt_send.at[0], cnt_recv.at[member], 1).wait_recv()
    total = cnt[0]
    for m in range(1, G):
        total = total + cnt[m]
    wide = jnp.concatenate(
        [jnp.transpose(jnp.broadcast_to(total[0:1, h : h + 128], (128, 128))) for h in range(0, points, 128)],
        axis=0,
    )
    deg = jnp.concatenate([wide] * (feat // 128), axis=1) + 1.0
    degree[...] = deg
    scale[...] = (cot_ref[...] / deg).astype(BF16).astype(F32)

    @pl.when(r % C != c)
    def _():
        for n in range(1, R):
            fh_copy(n).start()

    e_acc[...] = jnp.zeros_like(e_acc)
    f_acc[...] = jnp.zeros_like(f_acc)

    lane_m = lax.broadcasted_iota(jnp.int32, (16, LANES * B), 1) // B
    near_mask = jnp.where(
        lax.broadcasted_iota(jnp.int32, (16, LANES * B), 0) == lane_m, 1.0, 0.0
    ).astype(BF16)
    eye_mask = jnp.where(
        lax.broadcasted_iota(jnp.int32, (B, LANES * B), 1) % B
        == lax.broadcasted_iota(jnp.int32, (B, LANES * B), 0),
        1.0,
        0.0,
    ).astype(BF16)

    def in_order(ref):
        return jnp.concatenate(
            [
                jnp.concatenate([ref[k, pl.ds(m, step, stride=8), :] for m in range(LANES)], axis=0)
                for k in range(feat // 128)
            ],
            axis=1,
        )

    def chosen(block, n, value):
        return jnp.where(jnp.full(value.shape, block, jnp.int32) == n, value, 0.0)

    def picked(ref, block):
        value = chosen(block, 0, ref[0:B, :])
        for n in range(1, nblk):
            value = value + chosen(block, n, ref[n * B : (n + 1) * B, :])
        return value

    def section(u):
        owner = u * C + c

        @pl.when(owner != r)
        def _():
            fh_wait(owner)

        npanel[...] = dot(fh_all[own_rows(owner), :], wn_ref[...]).astype(BF16).astype(F32) * 0.5

        for q in range(Q):
            t = u * Q + q
            row_block = rows_s[t] - r * nblk
            col_block = cols_s[t] % nblk
            nval = picked(npanel, col_block).astype(BF16).reshape(B // 16, 16, feat)
            far_acc[...] = jnp.zeros_like(far_acc)
            c_tile[...] = picked(center, row_block)
            s_tile[...] = picked(scale, row_block) * 0.5

            def group(g, carry):
                sil, slo = [], []
                for m in range(LANES):
                    at = pl.ds(g + m * step, 1)
                    crow = jnp.broadcast_to(c_tile[at, :], (16, feat)).astype(BF16)
                    srow = jnp.broadcast_to(s_tile[at, :], (16, feat)).astype(BF16)
                    h = nval + crow[None]
                    th = jnp.tanh(h)
                    one = 1.0 + th
                    sil.append((h * one).reshape(B, feat))
                    slo.append((one * (1.0 + h * (1.0 - th)) * srow[None]).reshape(B, feat))
                sil = jnp.concatenate(sil, axis=0)
                slo = jnp.concatenate(slo, axis=0)
                arow = jnp.broadcast_to(a4_ref[t, pl.ds(g, 1), :], (16, LANES * B)).astype(BF16)
                near_l = near_mask * arow
                far_l = (eye_mask.reshape(B // 16, 16, LANES * B) * arow[None]).reshape(B, LANES * B)
                out_s = dot(near_l, sil)
                out_d = dot(jnp.concatenate([near_l, far_l], axis=0), slo)
                at8 = pl.ds(pl.multiple_of(g * 8, 8), 8)
                for k in range(feat // 128):
                    near_s[k, at8, :] = out_s[0:8, k * 128 : (k + 1) * 128]
                    near_d[k, at8, :] = out_d[0:8, k * 128 : (k + 1) * 128]
                far_acc[...] += out_d[16:]
                return carry

            lax.fori_loop(0, step, group, 0, unroll=4)
            tile_e, tile_c = in_order(near_s), in_order(near_d)
            far = far_acc[...]
            for n in range(nblk):
                block = slice(n * B, (n + 1) * B)
                e_acc[0, block, :] += chosen(row_block, n, tile_e)
                e_acc[1, block, :] += chosen(row_block, n, tile_c)
                if q == 0:
                    f_acc[block, :] = chosen(col_block, n, far)
                else:
                    f_acc[block, :] += chosen(col_block, n, far)

        far_out[u] = f_acc[...].astype(BF16)

        def far_copy(n):
            member = (p + n) % G
            return member_copy(
                far_out.at[u, slice_rows(member)],
                far_in.at[r * S + s],
                far_send.at[u * G + n],
                far_recv.at[r * S + s],
                n,
                owner,
            )

        for n in range(1, G):
            far_copy(n).start()

        @pl.when(owner != r)
        def _():
            far_copy(0).start()

        @pl.when(owner == r)
        def _():
            far_in[pl.ds(r * S + s, 1)] = far_out[u, slice_rows(p), :][None]

        return far_copy

    far_copies = [section(u) for u in range(U)]

    near_out[...] = e_acc[...].astype(BF16)
    near_copies = [
        member_copy(
            near_out.at[:, slice_rows((p + n) % G)],
            near_in.at[p],
            near_send.at[n],
            near_recv.at[p],
            n,
        )
        for n in range(1, G)
    ]
    for copy in near_copies:
        copy.start()

    mine = slice_rows(p)
    cs, ns = center[mine, :], nown[mine, :]
    sc, dg = scale[mine, :], degree[mine, :]
    self_h = cs + ns
    self_t = jnp.tanh(self_h)
    self_silu = self_h * (1.0 + self_t)
    self_slope = sc * 0.5 * (1.0 + self_t) * (1.0 + self_h * (1.0 - self_t))
    e_sum = e_acc[0, mine, :] + self_silu
    c_sum = e_acc[1, mine, :] + self_slope
    for n in range(1, G):
        member = (p + n) % G
        member_copy(
            near_out.at[:, mine], near_in.at[member], near_send.at[0], near_recv.at[member], 1
        ).wait_recv()
        arrived = near_in[pl.ds(member, 1)][0]
        e_sum = e_sum + arrived[0].astype(F32)
        c_sum = c_sum + arrived[1].astype(F32)
    eo_all[mine, :] = (e_sum / dg).astype(BF16)
    eo_copies = [
        member_copy(eo_all.at[mine], eo_all.at[mine], eo_send.at[n], eo_recv.at[p], n)
        for n in range(1, G)
    ]
    for copy in eo_copies:
        copy.start()

    n_sum = self_slope
    for row in range(R):
        for sub in range(S):
            slot = row * S + sub
            here = (row == r) & (sub == s) & (r % C == c)

            @pl.when(jnp.logical_not(here))
            def _():
                member_copy(
                    far_out.at[0, mine], far_in.at[slot], far_send.at[0], far_recv.at[slot], 1
                ).wait_recv()

            n_sum = n_sum + far_in[slot].astype(F32)

    def own_part(owner, member):
        return halves.at[:, hall_rows(owner, member)]

    halves[0, hall_rows(r, p), :] = c_sum.astype(BF16)
    halves[1, hall_rows(r, p), :] = n_sum.astype(BF16)

    def row_copy(n):
        return pltpu.make_async_remote_copy(
            src_ref=own_part(r, p),
            dst_ref=own_part(r, p),
            send_sem=row_send.at[n],
            recv_sem=row_recv.at[r],
            device_id=dev((r + n) % R, p),
            device_id_type=MESH,
        )

    def part_wait(owner, member, sems, at):
        pltpu.make_async_remote_copy(
            src_ref=own_part(owner, member),
            dst_ref=own_part(owner, member),
            send_sem=row_send.at[0],
            recv_sem=sems.at[at],
            device_id=dev(r, p),
            device_id_type=MESH,
        ).wait_recv()

    def part_copy(n_row, n, via, chips, cores):
        owner = (r + n_row) % R
        member = ((c + via) % C) * S + s
        return pltpu.make_async_remote_copy(
            src_ref=own_part(owner, member),
            dst_ref=own_part(owner, member),
            send_sem=grp_send.at[n_row * G + n],
            recv_sem=grp_recv.at[owner * G + member],
            device_id=(t_id, r, (c + chips) % C, (s + cores) % S),
            device_id_type=MESH,
        )

    def across(n_row):
        return [part_copy(n_row, k - 1, 0, k, 0) for k in range(1, C)]

    def inside(n_row, via):
        return [part_copy(n_row, C + via * (S - 1) + k - 2, via, 0, k) for k in range(1, S)]

    for n in range(1, R):
        row_copy(n).start()
    for copy in across(0) + inside(0, 0):
        copy.start()
    for n_row in range(R):
        owner = (r + n_row) % R
        if n_row > 0:
            part_wait(owner, p, row_recv, owner)
            for copy in across(n_row) + inside(n_row, 0):
                copy.start()
        before = n_row - 1
        if before >= 0:
            owner = (r + before) % R
            for via in range(1, C):
                member = ((c + via) % C) * S + s
                part_wait(owner, member, grp_recv, owner * G + member)
                for copy in inside(before, via):
                    copy.start()
    last = (r + R - 1) % R
    for via in range(1, C):
        member = ((c + via) % C) * S + s
        part_wait(last, member, grp_recv, last * G + member)
        for copy in inside(R - 1, via):
            copy.start()

    for n in range(1, G):
        member = (p + n) % G
        rows = slice_rows(member)
        member_copy(eo_all.at[rows], eo_all.at[rows], eo_send.at[0], eo_recv.at[member], 1).wait_recv()
    eo_ref[...] = eo_all[...].astype(F32)

    def grp_wait(owner):
        for via in range(C):
            for k in range(1, S):
                member = ((c + via) % C) * S + (s + k) % S
                part_wait(owner, member, grp_recv, owner * G + member)

    grp_wait(r)
    fg_ref[...] = dot(halves[0, own_rows(r), :], wc_ref[...], ((1,), (1,))) + dot(
        halves[1, own_rows(r), :], wn_ref[...], ((1,), (1,))
    )
    for n in range(1, R):
        owner = (r + n) % R

        @pl.when(owner % C != c)
        def _():
            fh_wait(owner)

    for n in range(1, R):
        grp_wait((r + n) % R)
    cg_ref[...] = dot(fh_all[...], halves[0], ((0,), (0,)))
    ng_ref[...] = dot(fh_all[...], halves[1], ((0,), (0,)))

    for n in range(1, R):
        fh_copy(n).wait_send()
        row_copy(n).wait_send()
    for copy in cnt_copies + near_copies + eo_copies:
        copy.wait_send()
    for n_row in range(R):
        for copy in across(n_row) + [one for via in range(C) for one in inside(n_row, via)]:
            copy.wait_send()
    for u in range(U):
        for n in range(1, G):
            far_copies[u](n).wait_send()

        @pl.when(u * C + c != r)
        def _():
            far_copies[u](0).wait_send()


def body(features, center_weight, neighbor_weight, cotangent, tile_rows, tile_cols, tile_links):
    R, C, S = lax.axis_size("rows"), lax.axis_size("rep"), lax.axis_size("sub")
    U = R // C
    T, B = tile_rows.shape[0], tile_links.shape[1]
    points, feat = features.shape
    G = C * S
    sl = points // G
    sizes = (R, C, S, U, T // U, B)
    step = B // LANES
    dma = pltpu.SemaphoreType.DMA
    vm = pltpu.VMEM
    out = jax.ShapeDtypeStruct
    return pl.pallas_call(
        functools.partial(kernel, sizes),
        out_shape=(
            out((points, feat), F32),
            out((points, feat), F32),
            out((feat, feat), F32),
            out((feat, feat), F32),
        ),
        in_specs=[pl.BlockSpec(memory_space=pltpu.HBM)] * 7,
        out_specs=[pl.BlockSpec(memory_space=pltpu.VMEM)] * 4,
        scratch_shapes=[
            pltpu.SMEM((T,), jnp.int32),
            pltpu.SMEM((T,), jnp.int32),
            vm((points, feat), F32),
            vm((feat, feat), BF16),
            vm((feat, feat), BF16),
            vm((points, feat), F32),
            vm((T, B, B), jnp.int32),
            dma((7,)),
            vm((R * points, feat), BF16),
            vm((2, R * points, feat), BF16),
            vm((points, feat), F32),
            vm((points, feat), F32),
            vm((points, feat), F32),
            vm((points, feat), F32),
            vm((points, feat), F32),
            vm((T, step, LANES * B), F32),
            vm((feat // 128, step * 8, 128), F32),
            vm((feat // 128, step * 8, 128), F32),
            vm((B, feat), F32),
            vm((B, feat), F32),
            vm((B, feat), F32),
            vm((2, points, feat), F32),
            vm((points, feat), F32),
            vm((2, points, feat), BF16),
            vm((U, points, feat), BF16),
            vm((G, 2, sl, feat), BF16),
            vm((R * S, sl, feat), BF16),
            vm((G, 8, points), F32),
            vm((points, feat), BF16),
            dma((R,)),
            dma((R,)),
            dma((G,)),
            dma((G,)),
            dma((G,)),
            dma((G,)),
            dma((U * G,)),
            dma((R * S,)),
            dma((R,)),
            dma((R,)),
            dma((R * G,)),
            dma((R * G,)),
            dma((G,)),
            dma((G,)),
        ],
        compiler_params=pltpu.CompilerParams(
            collective_id=0, has_side_effects=True
        ),
    )(tile_rows, tile_cols, features, center_weight, neighbor_weight, cotangent, tile_links)


def solution(mesh):
    in_specs = (
        P(("tiles", "rows"), None),
        P(),
        P(),
        P(("tiles", "rows"), None),
        P(("tiles", "rows", "rep", "sub")),
        P(("tiles", "rows", "rep", "sub")),
        P(("tiles", "rows", "rep", "sub"), None, None),
    )
    out_specs = (
        P(("tiles", "rows"), None),
        P(("tiles", "rows"), None),
        P("tiles", None),
        P("tiles", None),
    )
    return jax.shard_map(body, mesh=mesh, in_specs=in_specs, out_specs=out_specs, check_vma=False)
```

```python
import functools

import jax
import jax.numpy as jnp
from jax import lax
from jax.experimental import pallas as pl
from jax.experimental.pallas import tpu as pltpu
from jax.sharding import PartitionSpec as P

F32 = jnp.float32
BF16 = jnp.bfloat16
MESH = pl.DeviceIdType.MESH
LANES = 4


def dot(a, b, dims=((1,), (0,))):
    return lax.dot_general(a, b, (dims, ((), ())), preferred_element_type=F32)


def kernel(
    sizes,
    rows_h,
    cols_h,
    feat_h,
    wc_h,
    wn_h,
    cot_h,
    links_h,
    eo_ref,
    fg_ref,
    cg_ref,
    ng_ref,
    rows_s,
    cols_s,
    feat_ref,
    wc_ref,
    wn_ref,
    cot_ref,
    links_ref,
    in_sem,
    fh_all,
    halves,
    center,
    nown,
    scale,
    degree,
    npanel,
    a4_ref,
    near_s,
    near_d,
    far_acc,
    c_tile,
    s_tile,
    e_acc,
    f_acc,
    near_out,
    far_out,
    near_in,
    far_in,
    cnt,
    eo_all,
    fh_send,
    fh_recv,
    cnt_send,
    cnt_recv,
    near_send,
    near_recv,
    far_send,
    far_recv,
    row_send,
    row_recv,
    grp_send,
    grp_recv,
    eo_send,
    eo_recv,
):
    R, C, S, U, Q, B = sizes
    G = C * S
    points, feat = feat_ref.shape
    nblk = points // B
    sl = points // G
    step = B // LANES
    t_id = lax.axis_index("tiles")
    r = lax.axis_index("rows")
    c = lax.axis_index("rep")
    s = lax.axis_index("sub")
    p = c * S + s

    def dev(row, member):
        return (t_id, row, member // S, member % S)

    loads = [
        pltpu.make_async_copy(src, dst, in_sem.at[k])
        for k, (src, dst) in enumerate(
            (
                (feat_h, feat_ref),
                (links_h, links_ref),
                (rows_h, rows_s),
                (cols_h, cols_s),
                (wc_h, wc_ref),
                (wn_h, wn_ref),
                (cot_h, cot_ref),
            )
        )
    ]
    for load in loads:
        load.start()

    barrier = pltpu.get_barrier_semaphore()

    def greet(n, carry):
        other = (r * G + p + n) % (R * G)
        row, member = other // G, other % G

        @pl.when((row == r) | (member == p) | (member // S == r % C))
        def _():
            pl.semaphore_signal(barrier, inc=1, device_id=dev(row, member), device_id_type=MESH)

        return carry

    lax.fori_loop(1, R * G, greet, 0)

    def own_rows(owner):
        return pl.ds(pl.multiple_of(owner * points, points), points)

    def slice_rows(member):
        return pl.ds(pl.multiple_of(member * sl, sl), sl)

    def hall_rows(owner, member):
        return pl.ds(pl.multiple_of(owner * points + member * sl, sl), sl)

    loads[0].wait()
    fh = feat_ref[...].astype(BF16)
    fh_all[own_rows(r), :] = fh

    for load in loads[1:4]:
        load.wait()

    count = [jnp.zeros((8, B), F32) for _ in range(nblk)]
    for t in range(U * Q):
        tile = links_ref[t].astype(F32)
        a4_ref[t] = jnp.concatenate([tile[m * step : (m + 1) * step] for m in range(LANES)], axis=1)
        row_sum = dot(jnp.ones((8, B), BF16), tile.astype(BF16), ((1,), (1,)))
        block = rows_s[t] - r * nblk
        count = [count[n] + jnp.where(jnp.full(row_sum.shape, block, jnp.int32) == n, row_sum, 0.0) for n in range(nblk)]
    cnt[pl.ds(p, 1)] = jnp.concatenate(count, axis=1)[None]

    far_rows = jnp.where(r % C == c, U - 1, U)
    pl.semaphore_wait(barrier, R - 1 + G - 1 + far_rows * (G - 1))

    def fh_copy(n):
        to = (r + n) % R
        return pltpu.make_async_remote_copy(
            src_ref=fh_all.at[own_rows(r)],
            dst_ref=fh_all.at[own_rows(r)],
            send_sem=fh_send.at[n],
            recv_sem=fh_recv.at[r],
            device_id=dev(to, p),
            device_id_type=MESH,
        )

    def fh_wait(owner):
        pltpu.make_async_remote_copy(
            src_ref=fh_all.at[own_rows(owner)],
            dst_ref=fh_all.at[own_rows(owner)],
            send_sem=fh_send.at[0],
            recv_sem=fh_recv.at[owner],
            device_id=dev(r, p),
            device_id_type=MESH,
        ).wait_recv()

    def member_copy(src, dst, send_sem, recv_sem, n, owner=None):
        return pltpu.make_async_remote_copy(
            src_ref=src,
            dst_ref=dst,
            send_sem=send_sem,
            recv_sem=recv_sem,
            device_id=dev(r if owner is None else owner, (p + n) % G),
            device_id_type=MESH,
        )

    cnt_copies = [
        member_copy(cnt.at[p], cnt.at[p], cnt_send.at[n], cnt_recv.at[p], n) for n in range(1, G)
    ]
    for copy in cnt_copies:
        copy.start()

    @pl.when(r % C == c)
    def _():
        for n in range(1, R):
            fh_copy(n).start()

    for load in loads[4:]:
        load.wait()
    cc = dot(fh, wc_ref[...]).astype(BF16).astype(F32) * 0.5
    center[...] = cc
    nn = dot(fh, wn_ref[...]).astype(BF16).astype(F32) * 0.5
    nown[...] = nn

    for n in range(1, G):
        member = (p + n) % G
        member_copy(cnt.at[member], cnt.at[member], cnt_send.at[0], cnt_recv.at[member], 1).wait_recv()
    total = cnt[0]
    for m in range(1, G):
        total = total + cnt[m]
    wide = jnp.concatenate(
        [jnp.transpose(jnp.broadcast_to(total[0:1, h : h + 128], (128, 128))) for h in range(0, points, 128)],
        axis=0,
    )
    deg = jnp.concatenate([wide] * (feat // 128), axis=1) + 1.0
    degree[...] = deg
    scale[...] = (cot_ref[...] / deg).astype(BF16).astype(F32)

    @pl.when(r % C != c)
    def _():
        for n in range(1, R):
            fh_copy(n).start()

    e_acc[...] = jnp.zeros_like(e_acc)
    f_acc[...] = jnp.zeros_like(f_acc)

    lane_m = lax.broadcasted_iota(jnp.int32, (16, LANES * B), 1) // B
    near_mask = jnp.where(
        lax.broadcasted_iota(jnp.int32, (16, LANES * B), 0) == lane_m, 1.0, 0.0
    ).astype(BF16)
    eye_mask = jnp.where(
        lax.broadcasted_iota(jnp.int32, (B, LANES * B), 1) % B
        == lax.broadcasted_iota(jnp.int32, (B, LANES * B), 0),
        1.0,
        0.0,
    ).astype(BF16)

    def in_order(ref):
        return jnp.concatenate(
            [
                jnp.concatenate([ref[k, pl.ds(m, step, stride=8), :] for m in range(LANES)], axis=0)
                for k in range(feat // 128)
            ],
            axis=1,
        )

    def chosen(block, n, value):
        return jnp.where(jnp.full(value.shape, block, jnp.int32) == n, value, 0.0)

    def picked(ref, block):
        value = chosen(block, 0, ref[0:B, :])
        for n in range(1, nblk):
            value = value + chosen(block, n, ref[n * B : (n + 1) * B, :])
        return value

    def section(u):
        owner = u * C + c

        @pl.when(owner != r)
        def _():
            fh_wait(owner)

        npanel[...] = dot(fh_all[own_rows(owner), :], wn_ref[...]).astype(BF16).astype(F32) * 0.5

        for q in range(Q):
            t = u * Q + q
            row_block = rows_s[t] - r * nblk
            col_block = cols_s[t] % nblk
            nval = picked(npanel, col_block).astype(BF16).reshape(B // 16, 16, feat)
            far_acc[...] = jnp.zeros_like(far_acc)
            c_tile[...] = picked(center, row_block)
            s_tile[...] = picked(scale, row_block) * 0.5

            def group(g, carry):
                sil, slo = [], []
                for m in range(LANES):
                    at = pl.ds(g + m * step, 1)
                    crow = jnp.broadcast_to(c_tile[at, :], (16, feat)).astype(BF16)
                    srow = jnp.broadcast_to(s_tile[at, :], (16, feat)).astype(BF16)
                    h = nval + crow[None]
                    th = jnp.tanh(h)
                    one = 1.0 + th
                    sil.append((h * one).reshape(B, feat))
                    slo.append((one * (1.0 + h * (1.0 - th)) * srow[None]).reshape(B, feat))
                sil = jnp.concatenate(sil, axis=0)
                slo = jnp.concatenate(slo, axis=0)
                arow = jnp.broadcast_to(a4_ref[t, pl.ds(g, 1), :], (16, LANES * B)).astype(BF16)
                near_l = near_mask * arow
                far_l = (eye_mask.reshape(B // 16, 16, LANES * B) * arow[None]).reshape(B, LANES * B)
                out_s = dot(near_l, sil)
                out_d = dot(jnp.concatenate([near_l, far_l], axis=0), slo)
                at8 = pl.ds(pl.multiple_of(g * 8, 8), 8)
                for k in range(feat // 128):
                    near_s[k, at8, :] = out_s[0:8, k * 128 : (k + 1) * 128]
                    near_d[k, at8, :] = out_d[0:8, k * 128 : (k + 1) * 128]
                far_acc[...] += out_d[16:]
                return carry

            lax.fori_loop(0, step, group, 0, unroll=8)
            tile_e, tile_c = in_order(near_s), in_order(near_d)
            far = far_acc[...]
            for n in range(nblk):
                block = slice(n * B, (n + 1) * B)
                e_acc[0, block, :] += chosen(row_block, n, tile_e)
                e_acc[1, block, :] += chosen(row_block, n, tile_c)
                if q == 0:
                    f_acc[block, :] = chosen(col_block, n, far)
                else:
                    f_acc[block, :] += chosen(col_block, n, far)

        far_out[u] = f_acc[...].astype(BF16)

        def far_copy(n):
            member = (p + n) % G
            return member_copy(
                far_out.at[u, slice_rows(member)],
                far_in.at[r * S + s],
                far_send.at[u * G + n],
                far_recv.at[r * S + s],
                n,
                owner,
            )

        for n in range(1, G):
            far_copy(n).start()

        @pl.when(owner != r)
        def _():
            far_copy(0).start()

        @pl.when(owner == r)
        def _():
            far_in[pl.ds(r * S + s, 1)] = far_out[u, slice_rows(p), :][None]

        return far_copy

    far_copies = [section(u) for u in range(U)]

    near_out[...] = e_acc[...].astype(BF16)
    near_copies = [
        member_copy(
            near_out.at[:, slice_rows((p + n) % G)],
            near_in.at[p],
            near_send.at[n],
            near_recv.at[p],
            n,
        )
        for n in range(1, G)
    ]
    for copy in near_copies:
        copy.start()

    mine = slice_rows(p)
    cs, ns = center[mine, :], nown[mine, :]
    sc, dg = scale[mine, :], degree[mine, :]
    self_h = cs + ns
    self_t = jnp.tanh(self_h)
    self_silu = self_h * (1.0 + self_t)
    self_slope = sc * 0.5 * (1.0 + self_t) * (1.0 + self_h * (1.0 - self_t))
    e_sum = e_acc[0, mine, :] + self_silu
    c_sum = e_acc[1, mine, :] + self_slope
    for n in range(1, G):
        member = (p + n) % G
        member_copy(
            near_out.at[:, mine], near_in.at[member], near_send.at[0], near_recv.at[member], 1
        ).wait_recv()
        arrived = near_in[pl.ds(member, 1)][0]
        e_sum = e_sum + arrived[0].astype(F32)
        c_sum = c_sum + arrived[1].astype(F32)
    eo_all[mine, :] = (e_sum / dg).astype(BF16)
    eo_copies = [
        member_copy(eo_all.at[mine], eo_all.at[mine], eo_send.at[n], eo_recv.at[p], n)
        for n in range(1, G)
    ]
    for copy in eo_copies:
        copy.start()

    n_sum = self_slope
    for row in range(R):
        for sub in range(S):
            slot = row * S + sub
            here = (row == r) & (sub == s) & (r % C == c)

            @pl.when(jnp.logical_not(here))
            def _():
                member_copy(
                    far_out.at[0, mine], far_in.at[slot], far_send.at[0], far_recv.at[slot], 1
                ).wait_recv()

            n_sum = n_sum + far_in[slot].astype(F32)

    def own_part(owner, member):
        return halves.at[:, hall_rows(owner, member)]

    halves[0, hall_rows(r, p), :] = c_sum.astype(BF16)
    halves[1, hall_rows(r, p), :] = n_sum.astype(BF16)

    def row_copy(n):
        return pltpu.make_async_remote_copy(
            src_ref=own_part(r, p),
            dst_ref=own_part(r, p),
            send_sem=row_send.at[n],
            recv_sem=row_recv.at[r],
            device_id=dev((r + n) % R, p),
            device_id_type=MESH,
        )

    def part_wait(owner, member, sems, at):
        pltpu.make_async_remote_copy(
            src_ref=own_part(owner, member),
            dst_ref=own_part(owner, member),
            send_sem=row_send.at[0],
            recv_sem=sems.at[at],
            device_id=dev(r, p),
            device_id_type=MESH,
        ).wait_recv()

    def part_copy(n_row, n, via, chips, cores):
        owner = (r + n_row) % R
        member = ((c + via) % C) * S + s
        return pltpu.make_async_remote_copy(
            src_ref=own_part(owner, member),
            dst_ref=own_part(owner, member),
            send_sem=grp_send.at[n_row * G + n],
            recv_sem=grp_recv.at[owner * G + member],
            device_id=(t_id, r, (c + chips) % C, (s + cores) % S),
            device_id_type=MESH,
        )

    def across(n_row):
        return [part_copy(n_row, k - 1, 0, k, 0) for k in range(1, C)]

    def inside(n_row, via):
        return [part_copy(n_row, C + via * (S - 1) + k - 2, via, 0, k) for k in range(1, S)]

    for n in range(1, R):
        row_copy(n).start()
    for copy in across(0) + inside(0, 0):
        copy.start()
    for n_row in range(R):
        owner = (r + n_row) % R
        if n_row > 0:
            part_wait(owner, p, row_recv, owner)
            for copy in across(n_row) + inside(n_row, 0):
                copy.start()
        before = n_row - 1
        if before >= 0:
            owner = (r + before) % R
            for via in range(1, C):
                member = ((c + via) % C) * S + s
                part_wait(owner, member, grp_recv, owner * G + member)
                for copy in inside(before, via):
                    copy.start()
    last = (r + R - 1) % R
    for via in range(1, C):
        member = ((c + via) % C) * S + s
        part_wait(last, member, grp_recv, last * G + member)
        for copy in inside(R - 1, via):
            copy.start()

    for n in range(1, G):
        member = (p + n) % G
        rows = slice_rows(member)
        member_copy(eo_all.at[rows], eo_all.at[rows], eo_send.at[0], eo_recv.at[member], 1).wait_recv()
    eo_ref[...] = eo_all[...].astype(F32)

    def grp_wait(owner):
        for via in range(C):
            for k in range(1, S):
                member = ((c + via) % C) * S + (s + k) % S
                part_wait(owner, member, grp_recv, owner * G + member)

    grp_wait(r)
    fg_ref[...] = dot(halves[0, own_rows(r), :], wc_ref[...], ((1,), (1,))) + dot(
        halves[1, own_rows(r), :], wn_ref[...], ((1,), (1,))
    )
    for n in range(1, R):
        owner = (r + n) % R

        @pl.when(owner % C != c)
        def _():
            fh_wait(owner)

    for n in range(1, R):
        grp_wait((r + n) % R)
    cg_ref[...] = dot(fh_all[...], halves[0], ((0,), (0,)))
    ng_ref[...] = dot(fh_all[...], halves[1], ((0,), (0,)))

    for n in range(1, R):
        fh_copy(n).wait_send()
        row_copy(n).wait_send()
    for copy in cnt_copies + near_copies + eo_copies:
        copy.wait_send()
    for n_row in range(R):
        for copy in across(n_row) + [one for via in range(C) for one in inside(n_row, via)]:
            copy.wait_send()
    for u in range(U):
        for n in range(1, G):
            far_copies[u](n).wait_send()

        @pl.when(u * C + c != r)
        def _():
            far_copies[u](0).wait_send()


def body(features, center_weight, neighbor_weight, cotangent, tile_rows, tile_cols, tile_links):
    R, C, S = lax.axis_size("rows"), lax.axis_size("rep"), lax.axis_size("sub")
    U = R // C
    T, B = tile_rows.shape[0], tile_links.shape[1]
    points, feat = features.shape
    G = C * S
    sl = points // G
    sizes = (R, C, S, U, T // U, B)
    step = B // LANES
    dma = pltpu.SemaphoreType.DMA
    vm = pltpu.VMEM
    out = jax.ShapeDtypeStruct
    return pl.pallas_call(
        functools.partial(kernel, sizes),
        out_shape=(
            out((points, feat), F32),
            out((points, feat), F32),
            out((feat, feat), F32),
            out((feat, feat), F32),
        ),
        in_specs=[pl.BlockSpec(memory_space=pltpu.HBM)] * 7,
        out_specs=[pl.BlockSpec(memory_space=pltpu.VMEM)] * 4,
        scratch_shapes=[
            pltpu.SMEM((T,), jnp.int32),
            pltpu.SMEM((T,), jnp.int32),
            vm((points, feat), F32),
            vm((feat, feat), BF16),
            vm((feat, feat), BF16),
            vm((points, feat), F32),
            vm((T, B, B), jnp.int32),
            dma((7,)),
            vm((R * points, feat), BF16),
            vm((2, R * points, feat), BF16),
            vm((points, feat), F32),
            vm((points, feat), F32),
            vm((points, feat), F32),
            vm((points, feat), F32),
            vm((points, feat), F32),
            vm((T, step, LANES * B), F32),
            vm((feat // 128, step * 8, 128), F32),
            vm((feat // 128, step * 8, 128), F32),
            vm((B, feat), F32),
            vm((B, feat), F32),
            vm((B, feat), F32),
            vm((2, points, feat), F32),
            vm((points, feat), F32),
            vm((2, points, feat), BF16),
            vm((U, points, feat), BF16),
            vm((G, 2, sl, feat), BF16),
            vm((R * S, sl, feat), BF16),
            vm((G, 8, points), F32),
            vm((points, feat), BF16),
            dma((R,)),
            dma((R,)),
            dma((G,)),
            dma((G,)),
            dma((G,)),
            dma((G,)),
            dma((U * G,)),
            dma((R * S,)),
            dma((R,)),
            dma((R,)),
            dma((R * G,)),
            dma((R * G,)),
            dma((G,)),
            dma((G,)),
        ],
        compiler_params=pltpu.CompilerParams(
            collective_id=0, has_side_effects=True
        ),
    )(tile_rows, tile_cols, features, center_weight, neighbor_weight, cotangent, tile_links)


def solution(mesh):
    in_specs = (
        P(("tiles", "rows"), None),
        P(),
        P(),
        P(("tiles", "rows"), None),
        P(("tiles", "rows", "rep", "sub")),
        P(("tiles", "rows", "rep", "sub")),
        P(("tiles", "rows", "rep", "sub"), None, None),
    )
    out_specs = (
        P(("tiles", "rows"), None),
        P(("tiles", "rows"), None),
        P("tiles", None),
        P("tiles", None),
    )
    return jax.shard_map(body, mesh=mesh, in_specs=in_specs, out_specs=out_specs, check_vma=False)
```

```python
import functools

import jax
import jax.numpy as jnp
from jax import lax
from jax.experimental import pallas as pl
from jax.experimental.pallas import tpu as pltpu
from jax.sharding import PartitionSpec as P

F32 = jnp.float32
BF16 = jnp.bfloat16
MESH = pl.DeviceIdType.MESH
LANES = 4


def dot(a, b, dims=((1,), (0,))):
    return lax.dot_general(a, b, (dims, ((), ())), preferred_element_type=F32)


def kernel(
    sizes,
    rows_h,
    cols_h,
    feat_h,
    wc_h,
    wn_h,
    cot_h,
    links_h,
    eo_ref,
    fg_ref,
    cg_ref,
    ng_ref,
    rows_s,
    cols_s,
    feat_ref,
    wc_ref,
    wn_ref,
    cot_ref,
    links_ref,
    in_sem,
    fh_all,
    halves,
    center,
    nown,
    scale,
    degree,
    npanel,
    a4_ref,
    near_s,
    near_d,
    far_acc,
    c_tile,
    s_tile,
    e_acc,
    f_acc,
    near_out,
    far_out,
    near_in,
    far_in,
    cnt,
    eo_all,
    fh_send,
    fh_recv,
    cnt_send,
    cnt_recv,
    near_send,
    near_recv,
    far_send,
    far_recv,
    row_send,
    row_recv,
    grp_send,
    grp_recv,
    eo_send,
    eo_recv,
):
    R, C, S, U, Q, B = sizes
    G = C * S
    points, feat = feat_ref.shape
    nblk = points // B
    sl = points // G
    step = B // LANES
    t_id = lax.axis_index("tiles")
    r = lax.axis_index("rows")
    c = lax.axis_index("rep")
    s = lax.axis_index("sub")
    p = c * S + s

    def dev(row, member):
        return (t_id, row, member // S, member % S)

    loads = [
        pltpu.make_async_copy(src, dst, in_sem.at[k])
        for k, (src, dst) in enumerate(
            (
                (feat_h, feat_ref),
                (links_h, links_ref),
                (rows_h, rows_s),
                (cols_h, cols_s),
                (wc_h, wc_ref),
                (wn_h, wn_ref),
                (cot_h, cot_ref),
            )
        )
    ]
    for load in loads:
        load.start()

    barrier = pltpu.get_barrier_semaphore()

    def greet(n, carry):
        other = (r * G + p + n) % (R * G)
        row, member = other // G, other % G

        @pl.when((row == r) | (member == p) | (member // S == r % C))
        def _():
            pl.semaphore_signal(barrier, inc=1, device_id=dev(row, member), device_id_type=MESH)

        return carry

    lax.fori_loop(1, R * G, greet, 0)

    def own_rows(owner):
        return pl.ds(pl.multiple_of(owner * points, points), points)

    def slice_rows(member):
        return pl.ds(pl.multiple_of(member * sl, sl), sl)

    def hall_rows(owner, member):
        return pl.ds(pl.multiple_of(owner * points + member * sl, sl), sl)

    loads[0].wait()
    fh = feat_ref[...].astype(BF16)
    fh_all[own_rows(r), :] = fh

    for load in loads[1:4]:
        load.wait()

    count = [jnp.zeros((8, B), F32) for _ in range(nblk)]
    for t in range(U * Q):
        tile = links_ref[t].astype(F32)
        a4_ref[t] = jnp.concatenate([tile[m * step : (m + 1) * step] for m in range(LANES)], axis=1)
        row_sum = dot(jnp.ones((8, B), BF16), tile.astype(BF16), ((1,), (1,)))
        block = rows_s[t] - r * nblk
        count = [count[n] + jnp.where(jnp.full(row_sum.shape, block, jnp.int32) == n, row_sum, 0.0) for n in range(nblk)]
    cnt[pl.ds(p, 1)] = jnp.concatenate(count, axis=1)[None]

    far_rows = jnp.where(r % C == c, U - 1, U)
    pl.semaphore_wait(barrier, R - 1 + G - 1 + far_rows * (G - 1))

    def fh_copy(n):
        to = (r + n) % R
        return pltpu.make_async_remote_copy(
            src_ref=fh_all.at[own_rows(r)],
            dst_ref=fh_all.at[own_rows(r)],
            send_sem=fh_send.at[n],
            recv_sem=fh_recv.at[r],
            device_id=dev(to, p),
            device_id_type=MESH,
        )

    def fh_wait(owner):
        pltpu.make_async_remote_copy(
            src_ref=fh_all.at[own_rows(owner)],
            dst_ref=fh_all.at[own_rows(owner)],
            send_sem=fh_send.at[0],
            recv_sem=fh_recv.at[owner],
            device_id=dev(r, p),
            device_id_type=MESH,
        ).wait_recv()

    def member_copy(src, dst, send_sem, recv_sem, n, owner=None):
        return pltpu.make_async_remote_copy(
            src_ref=src,
            dst_ref=dst,
            send_sem=send_sem,
            recv_sem=recv_sem,
            device_id=dev(r if owner is None else owner, (p + n) % G),
            device_id_type=MESH,
        )

    cnt_copies = [
        member_copy(cnt.at[p], cnt.at[p], cnt_send.at[n], cnt_recv.at[p], n) for n in range(1, G)
    ]
    for copy in cnt_copies:
        copy.start()

    @pl.when(r % C == c)
    def _():
        for n in range(1, R):
            fh_copy(n).start()

    for load in loads[4:]:
        load.wait()
    cc = dot(fh, wc_ref[...]).astype(BF16).astype(F32) * 0.5
    center[...] = cc
    nn = dot(fh, wn_ref[...]).astype(BF16).astype(F32) * 0.5
    nown[...] = nn

    for n in range(1, G):
        member = (p + n) % G
        member_copy(cnt.at[member], cnt.at[member], cnt_send.at[0], cnt_recv.at[member], 1).wait_recv()
    total = cnt[0]
    for m in range(1, G):
        total = total + cnt[m]
    wide = jnp.concatenate(
        [jnp.transpose(jnp.broadcast_to(total[0:1, h : h + 128], (128, 128))) for h in range(0, points, 128)],
        axis=0,
    )
    deg = jnp.concatenate([wide] * (feat // 128), axis=1) + 1.0
    degree[...] = deg
    scale[...] = (cot_ref[...] / deg).astype(BF16).astype(F32)

    @pl.when(r % C != c)
    def _():
        for n in range(1, R):
            fh_copy(n).start()

    e_acc[...] = jnp.zeros_like(e_acc)
    f_acc[...] = jnp.zeros_like(f_acc)

    lane_m = lax.broadcasted_iota(jnp.int32, (16, LANES * B), 1) // B
    near_mask = jnp.where(
        lax.broadcasted_iota(jnp.int32, (16, LANES * B), 0) == lane_m, 1.0, 0.0
    ).astype(BF16)
    eye_mask = jnp.where(
        lax.broadcasted_iota(jnp.int32, (B, LANES * B), 1) % B
        == lax.broadcasted_iota(jnp.int32, (B, LANES * B), 0),
        1.0,
        0.0,
    ).astype(BF16)

    def in_order(ref):
        return jnp.concatenate(
            [
                jnp.concatenate([ref[k, pl.ds(m, step, stride=8), :] for m in range(LANES)], axis=0)
                for k in range(feat // 128)
            ],
            axis=1,
        )

    def chosen(block, n, value):
        return jnp.where(jnp.full(value.shape, block, jnp.int32) == n, value, 0.0)

    def picked(ref, block):
        value = chosen(block, 0, ref[0:B, :])
        for n in range(1, nblk):
            value = value + chosen(block, n, ref[n * B : (n + 1) * B, :])
        return value

    def section(u):
        owner = u * C + c

        @pl.when(owner != r)
        def _():
            fh_wait(owner)

        npanel[...] = dot(fh_all[own_rows(owner), :], wn_ref[...]).astype(BF16).astype(F32) * 0.5

        for q in range(Q):
            t = u * Q + q
            row_block = rows_s[t] - r * nblk
            col_block = cols_s[t] % nblk
            nval = picked(npanel, col_block).astype(BF16).reshape(B // 16, 16, feat)
            far_acc[...] = jnp.zeros_like(far_acc)
            c_tile[...] = picked(center, row_block)
            s_tile[...] = picked(scale, row_block) * 0.5

            def group(g, carry):
                sil, slo = [], []
                for m in range(LANES):
                    at = pl.ds(g + m * step, 1)
                    crow = jnp.broadcast_to(c_tile[at, :], (16, feat)).astype(BF16)
                    srow = jnp.broadcast_to(s_tile[at, :], (16, feat)).astype(BF16)
                    h = nval + crow[None]
                    th = jnp.tanh(h)
                    one = 1.0 + th
                    sil.append((h * one).reshape(B, feat))
                    slo.append((one * (1.0 + h * (1.0 - th)) * srow[None]).reshape(B, feat))
                sil = jnp.concatenate(sil, axis=0)
                slo = jnp.concatenate(slo, axis=0)
                arow = jnp.broadcast_to(a4_ref[t, pl.ds(g, 1), :], (16, LANES * B)).astype(BF16)
                near_l = near_mask * arow
                far_l = (eye_mask.reshape(B // 16, 16, LANES * B) * arow[None]).reshape(B, LANES * B)
                out_s = dot(near_l, sil)
                out_d = dot(jnp.concatenate([near_l, far_l], axis=0), slo)
                at8 = pl.ds(pl.multiple_of(g * 8, 8), 8)
                for k in range(feat // 128):
                    near_s[k, at8, :] = out_s[0:8, k * 128 : (k + 1) * 128]
                    near_d[k, at8, :] = out_d[0:8, k * 128 : (k + 1) * 128]
                far_acc[...] += out_d[16:]
                return carry

            lax.fori_loop(0, step, group, 0, unroll=16)
            tile_e, tile_c = in_order(near_s), in_order(near_d)
            far = far_acc[...]
            for n in range(nblk):
                block = slice(n * B, (n + 1) * B)
                e_acc[0, block, :] += chosen(row_block, n, tile_e)
                e_acc[1, block, :] += chosen(row_block, n, tile_c)
                if q == 0:
                    f_acc[block, :] = chosen(col_block, n, far)
                else:
                    f_acc[block, :] += chosen(col_block, n, far)

        far_out[u] = f_acc[...].astype(BF16)

        def far_copy(n):
            member = (p + n) % G
            return member_copy(
                far_out.at[u, slice_rows(member)],
                far_in.at[r * S + s],
                far_send.at[u * G + n],
                far_recv.at[r * S + s],
                n,
                owner,
            )

        for n in range(1, G):
            far_copy(n).start()

        @pl.when(owner != r)
        def _():
            far_copy(0).start()

        @pl.when(owner == r)
        def _():
            far_in[pl.ds(r * S + s, 1)] = far_out[u, slice_rows(p), :][None]

        return far_copy

    far_copies = [section(u) for u in range(U)]

    near_out[...] = e_acc[...].astype(BF16)
    near_copies = [
        member_copy(
            near_out.at[:, slice_rows((p + n) % G)],
            near_in.at[p],
            near_send.at[n],
            near_recv.at[p],
            n,
        )
        for n in range(1, G)
    ]
    for copy in near_copies:
        copy.start()

    mine = slice_rows(p)
    cs, ns = center[mine, :], nown[mine, :]
    sc, dg = scale[mine, :], degree[mine, :]
    self_h = cs + ns
    self_t = jnp.tanh(self_h)
    self_silu = self_h * (1.0 + self_t)
    self_slope = sc * 0.5 * (1.0 + self_t) * (1.0 + self_h * (1.0 - self_t))
    e_sum = e_acc[0, mine, :] + self_silu
    c_sum = e_acc[1, mine, :] + self_slope
    for n in range(1, G):
        member = (p + n) % G
        member_copy(
            near_out.at[:, mine], near_in.at[member], near_send.at[0], near_recv.at[member], 1
        ).wait_recv()
        arrived = near_in[pl.ds(member, 1)][0]
        e_sum = e_sum + arrived[0].astype(F32)
        c_sum = c_sum + arrived[1].astype(F32)
    eo_all[mine, :] = (e_sum / dg).astype(BF16)
    eo_copies = [
        member_copy(eo_all.at[mine], eo_all.at[mine], eo_send.at[n], eo_recv.at[p], n)
        for n in range(1, G)
    ]
    for copy in eo_copies:
        copy.start()

    n_sum = self_slope
    for row in range(R):
        for sub in range(S):
            slot = row * S + sub
            here = (row == r) & (sub == s) & (r % C == c)

            @pl.when(jnp.logical_not(here))
            def _():
                member_copy(
                    far_out.at[0, mine], far_in.at[slot], far_send.at[0], far_recv.at[slot], 1
                ).wait_recv()

            n_sum = n_sum + far_in[slot].astype(F32)

    def own_part(owner, member):
        return halves.at[:, hall_rows(owner, member)]

    halves[0, hall_rows(r, p), :] = c_sum.astype(BF16)
    halves[1, hall_rows(r, p), :] = n_sum.astype(BF16)

    def row_copy(n):
        return pltpu.make_async_remote_copy(
            src_ref=own_part(r, p),
            dst_ref=own_part(r, p),
            send_sem=row_send.at[n],
            recv_sem=row_recv.at[r],
            device_id=dev((r + n) % R, p),
            device_id_type=MESH,
        )

    def part_wait(owner, member, sems, at):
        pltpu.make_async_remote_copy(
            src_ref=own_part(owner, member),
            dst_ref=own_part(owner, member),
            send_sem=row_send.at[0],
            recv_sem=sems.at[at],
            device_id=dev(r, p),
            device_id_type=MESH,
        ).wait_recv()

    def part_copy(n_row, n, via, chips, cores):
        owner = (r + n_row) % R
        member = ((c + via) % C) * S + s
        return pltpu.make_async_remote_copy(
            src_ref=own_part(owner, member),
            dst_ref=own_part(owner, member),
            send_sem=grp_send.at[n_row * G + n],
            recv_sem=grp_recv.at[owner * G + member],
            device_id=(t_id, r, (c + chips) % C, (s + cores) % S),
            device_id_type=MESH,
        )

    def across(n_row):
        return [part_copy(n_row, k - 1, 0, k, 0) for k in range(1, C)]

    def inside(n_row, via):
        return [part_copy(n_row, C + via * (S - 1) + k - 2, via, 0, k) for k in range(1, S)]

    for n in range(1, R):
        row_copy(n).start()
    for copy in across(0) + inside(0, 0):
        copy.start()
    for n_row in range(R):
        owner = (r + n_row) % R
        if n_row > 0:
            part_wait(owner, p, row_recv, owner)
            for copy in across(n_row) + inside(n_row, 0):
                copy.start()
        before = n_row - 1
        if before >= 0:
            owner = (r + before) % R
            for via in range(1, C):
                member = ((c + via) % C) * S + s
                part_wait(owner, member, grp_recv, owner * G + member)
                for copy in inside(before, via):
                    copy.start()
    last = (r + R - 1) % R
    for via in range(1, C):
        member = ((c + via) % C) * S + s
        part_wait(last, member, grp_recv, last * G + member)
        for copy in inside(R - 1, via):
            copy.start()

    for n in range(1, G):
        member = (p + n) % G
        rows = slice_rows(member)
        member_copy(eo_all.at[rows], eo_all.at[rows], eo_send.at[0], eo_recv.at[member], 1).wait_recv()
    eo_ref[...] = eo_all[...].astype(F32)

    def grp_wait(owner):
        for via in range(C):
            for k in range(1, S):
                member = ((c + via) % C) * S + (s + k) % S
                part_wait(owner, member, grp_recv, owner * G + member)

    grp_wait(r)
    fg_ref[...] = dot(halves[0, own_rows(r), :], wc_ref[...], ((1,), (1,))) + dot(
        halves[1, own_rows(r), :], wn_ref[...], ((1,), (1,))
    )
    for n in range(1, R):
        owner = (r + n) % R

        @pl.when(owner % C != c)
        def _():
            fh_wait(owner)

    for n in range(1, R):
        grp_wait((r + n) % R)
    cg_ref[...] = dot(fh_all[...], halves[0], ((0,), (0,)))
    ng_ref[...] = dot(fh_all[...], halves[1], ((0,), (0,)))

    for n in range(1, R):
        fh_copy(n).wait_send()
        row_copy(n).wait_send()
    for copy in cnt_copies + near_copies + eo_copies:
        copy.wait_send()
    for n_row in range(R):
        for copy in across(n_row) + [one for via in range(C) for one in inside(n_row, via)]:
            copy.wait_send()
    for u in range(U):
        for n in range(1, G):
            far_copies[u](n).wait_send()

        @pl.when(u * C + c != r)
        def _():
            far_copies[u](0).wait_send()


def body(features, center_weight, neighbor_weight, cotangent, tile_rows, tile_cols, tile_links):
    R, C, S = lax.axis_size("rows"), lax.axis_size("rep"), lax.axis_size("sub")
    U = R // C
    T, B = tile_rows.shape[0], tile_links.shape[1]
    points, feat = features.shape
    G = C * S
    sl = points // G
    sizes = (R, C, S, U, T // U, B)
    step = B // LANES
    dma = pltpu.SemaphoreType.DMA
    vm = pltpu.VMEM
    out = jax.ShapeDtypeStruct
    return pl.pallas_call(
        functools.partial(kernel, sizes),
        out_shape=(
            out((points, feat), F32),
            out((points, feat), F32),
            out((feat, feat), F32),
            out((feat, feat), F32),
        ),
        in_specs=[pl.BlockSpec(memory_space=pltpu.HBM)] * 7,
        out_specs=[pl.BlockSpec(memory_space=pltpu.VMEM)] * 4,
        scratch_shapes=[
            pltpu.SMEM((T,), jnp.int32),
            pltpu.SMEM((T,), jnp.int32),
            vm((points, feat), F32),
            vm((feat, feat), BF16),
            vm((feat, feat), BF16),
            vm((points, feat), F32),
            vm((T, B, B), jnp.int32),
            dma((7,)),
            vm((R * points, feat), BF16),
            vm((2, R * points, feat), BF16),
            vm((points, feat), F32),
            vm((points, feat), F32),
            vm((points, feat), F32),
            vm((points, feat), F32),
            vm((points, feat), F32),
            vm((T, step, LANES * B), F32),
            vm((feat // 128, step * 8, 128), F32),
            vm((feat // 128, step * 8, 128), F32),
            vm((B, feat), F32),
            vm((B, feat), F32),
            vm((B, feat), F32),
            vm((2, points, feat), F32),
            vm((points, feat), F32),
            vm((2, points, feat), BF16),
            vm((U, points, feat), BF16),
            vm((G, 2, sl, feat), BF16),
            vm((R * S, sl, feat), BF16),
            vm((G, 8, points), F32),
            vm((points, feat), BF16),
            dma((R,)),
            dma((R,)),
            dma((G,)),
            dma((G,)),
            dma((G,)),
            dma((G,)),
            dma((U * G,)),
            dma((R * S,)),
            dma((R,)),
            dma((R,)),
            dma((R * G,)),
            dma((R * G,)),
            dma((G,)),
            dma((G,)),
        ],
        compiler_params=pltpu.CompilerParams(
            collective_id=0, has_side_effects=True
        ),
    )(tile_rows, tile_cols, features, center_weight, neighbor_weight, cotangent, tile_links)


def solution(mesh):
    in_specs = (
        P(("tiles", "rows"), None),
        P(),
        P(),
        P(("tiles", "rows"), None),
        P(("tiles", "rows", "rep", "sub")),
        P(("tiles", "rows", "rep", "sub")),
        P(("tiles", "rows", "rep", "sub"), None, None),
    )
    out_specs = (
        P(("tiles", "rows"), None),
        P(("tiles", "rows"), None),
        P("tiles", None),
        P("tiles", None),
    )
    return jax.shard_map(body, mesh=mesh, in_specs=in_specs, out_specs=out_specs, check_vma=False)
```
